32 devices in a mesh: batch: 8 (over z, x), task: 4 (over y, core).
Axes of the slice: x: 2, y: 2, z: 4, core: 2. Of those that a mesh axis runs over, the one named last changes fastest.
Arguments:
- tokens: bfloat16 [2, 32, 1024, 1024], P(None, ('batch', 'task')), may hold values from -6 to 6
- cotangent: bfloat16 [2, 32, 1024, 1024], P(None, ('batch', 'task')), may hold values from -6 to 6
- segment_ids: int32 [2, 32, 1024], P(None, ('batch', 'task')), may hold values from 0 to 15, never falling along the last dimension, each value on 1 to 128 neighbouring positions
- task_ids: int32 [2, 32, 16], P(None, ('batch', 'task')), may hold values from 0 to 3
- ln1_gain: bfloat16 [1024], replicated, may hold values from 0.5 to 1.5
- ln1_bias: bfloat16 [1024], replicated, may hold values from -1.75 to 1.75
- w_qkv: bfloat16 [1024, 3072], replicated, may hold values from -0.1875 to 0.1875
- b_qkv: bfloat16 [3072], replicated, may hold values from -1.75 to 1.75
- w_attn_out: bfloat16 [1024, 1024], replicated, may hold values from -0.5 to 0.5
- b_attn_out: bfloat16 [1024], replicated, may hold values from -1.75 to 1.75
- ln2_gain: bfloat16 [1024], replicated, may hold values from 0.5 to 1.5
- ln2_bias: bfloat16 [1024], replicated, may hold values from -1.75 to 1.75
- w_fc: bfloat16 [1024, 4096], replicated, may hold values from -0.1875 to 0.1875
- b_fc: bfloat16 [4096], replicated, may hold values from -1.75 to 1.75
- w_proj: bfloat16 [4096, 1024], replicated, may hold values from -0.09375 to 0.09375
- b_proj: bfloat16 [1024], replicated, may hold values from -1.75 to 1.75
- prefix_embed: bfloat16 [4, 10, 1024], P('task'), may hold values from -6 to 6
- reparam_in: bfloat16 [4, 1024, 512], P('task'), may hold values from -0.1875 to 0.1875
- reparam_in_bias: bfloat16 [4, 512], P('task'), may hold values from -3 to 3
- reparam_out: bfloat16 [4, 512, 2048], P('task'), may hold values from -0.25 to 0.25
- reparam_out_bias: bfloat16 [4, 2048], P('task'), may hold values from -3 to 3
Outputs:
- block_out: bfloat16 [2, 32, 1024, 1024], P(None, ('batch', 'task'))
- input_grad: bfloat16 [2, 32, 1024, 1024], P(None, ('batch', 'task'))
- grad_prefix_embed: float32 [4, 10, 1024], P('task')
- grad_reparam_in: float32 [4, 1024, 512], P('task')
- grad_reparam_in_bias: float32 [4, 512], P('task')
- grad_reparam_out: float32 [4, 512, 2048], P('task')
- grad_reparam_out_bias: float32 [4, 2048], P('task')
The draws below stay inside these ranges and needn't reach their ends.
Inputs may be any that keep to these rules, and one draw needn't show every extreme that they name: `segment_ids`: in each row segment numbers never fall and each example holds 1 to 128 tokens; some example holds exactly 128.
All inputs are finite; a program needn't handle non-finite values.
Results may differ from the reference program's by a relative error of at most 0.02.
Values may be sent and summed in bfloat16 or wider, within the bound.
A program may use at most 448 MiB of HBM per device.

```python
import math
import jax
import jax.numpy as jnp
import numpy as np
from jax import lax

D = 1024
HEADS = 16
FF = 4096
RANK = 512
PREFIX = 10
SEQ = 1024
MOST = 128
SEGS = 16
MICRO = 2
TASKS = 4
ROWS = 32


def plant(array, stream_key, low, top_value):
    index_at = [jax.random.randint(jax.random.fold_in(stream_key, axis), (), 0, length) for axis, length in enumerate(array.shape)]
    main_axis = array.shape.index(max(array.shape))
    next_to = index_at[:main_axis] + [(index_at[main_axis] + 1) % array.shape[main_axis]] + index_at[main_axis + 1:]
    return array.at[tuple(index_at)].set(low).at[tuple(next_to)].set(top_value)


def block_levels(rng, dims, cuts, low, largest):
    loudness = 1.0
    for dim, blocks in cuts:
        steps = jax.random.uniform(jax.random.fold_in(jax.random.fold_in(rng, 6), dim), (blocks,), jnp.float32, low / len(cuts), largest / len(cuts))
        loudness = loudness * jnp.repeat(jnp.exp(steps), dims[dim] // blocks).reshape((-1,) + (1,) * (len(dims) - 1 - dim))
    return loudness


def split_up(amount, total, bound, slope):
    weights = [(1 << 20) // math.isqrt(grade ** slope) + 1 for grade in range(2, amount + 1)]
    surplus, holding = total - bound - (amount - 1), [1] * (amount - 1)
    while surplus > 0:
        candidates = [i for i in range(amount - 1) if holding[i] < bound]
        mass, remaining = sum([weights[i] for i in candidates]), surplus
        for i in candidates:
            addition = min(bound - holding[i], max(1, remaining * weights[i] // mass), surplus)
            holding[i] = holding[i] + addition
            surplus = surplus - addition
    return np.array([bound] + holding)


def ragged_sizes(own_key, number_of, total, most, skew):
    if number_of == 2:
        one = jax.random.randint(own_key, (), max(1, total - most), min(most, total - 1) + 1)
        return jnp.stack([one, total - one])
    lengths = jnp.asarray(split_up(number_of, total, most, skew), jnp.int32)
    pairs = (number_of - 1) // 2
    donor, receiver = lengths[1:1 + 2 * pairs:2], lengths[2:2 + 2 * pairs:2]
    margin = jnp.minimum(donor - 1, most - receiver)
    moved = jax.random.randint(jax.random.fold_in(own_key, 1), (pairs,), 0, 1 << 20) % (margin + 1)
    lengths = lengths.at[1:1 + 2 * pairs:2].set(donor - moved).at[2:2 + 2 * pairs:2].set(receiver + moved)
    return lengths[jax.random.permutation(jax.random.fold_in(own_key, 2), number_of)]


def gaussian(rng, extent, scale, bound, pieces=(), dtype=jnp.bfloat16):
    level = block_levels(rng, extent, pieces, -0.22, 0.18) if pieces else 1.0
    drawn = jax.random.normal(rng, extent, jnp.float32) * scale * level
    return jnp.minimum(jnp.maximum(drawn, -bound), bound).astype(dtype)


def setup_inputs(seed: int = 0) -> dict:
    key_of = jax.random.split(jax.random.key(seed), 22)
    tokens = gaussian(key_of[0], (MICRO, ROWS, SEQ, D), 1.0, 6.0, ((1, 32),))
    cotangent = gaussian(key_of[1], (MICRO, ROWS, SEQ, D), 1.0, 6.0, ((1, 32),))
    segment_ids = jax.vmap(lambda own: jnp.searchsorted(jnp.cumsum(ragged_sizes(own, SEGS, SEQ, MOST, 1)), jnp.arange(SEQ), side="right"))(jax.random.split(key_of[2], MICRO * ROWS)).reshape((MICRO, ROWS, SEQ)).astype(jnp.int32)
    task_ids = plant(jax.random.randint(key_of[3], (MICRO, ROWS, SEGS), 0, TASKS), jax.random.fold_in(key_of[3], 1), 0, TASKS - 1).astype(jnp.int32)
    ln1_gain = jnp.clip(1.0 + 0.1 * jax.random.normal(key_of[4], (D,), jnp.float32), 0.5, 1.5).astype(jnp.bfloat16)
    ln1_bias = gaussian(key_of[5], (D,), 0.3, 1.75)
    w_qkv = gaussian(key_of[6], (D, 3 * D), D ** -0.5, 0.1875)
    b_qkv = gaussian(key_of[7], (3 * D,), 0.3, 1.75)
    w_attn_out = gaussian(key_of[8], (D, D), (D // 8) ** -0.5, 0.5)
    b_attn_out = gaussian(key_of[9], (D,), 0.3, 1.75)
    ln2_gain = jnp.clip(1.0 + 0.1 * jax.random.normal(key_of[10], (D,), jnp.float32), 0.5, 1.5).astype(jnp.bfloat16)
    ln2_bias = gaussian(key_of[11], (D,), 0.3, 1.75)
    w_fc = gaussian(key_of[12], (D, FF), D ** -0.5, 0.1875)
    b_fc = gaussian(key_of[13], (FF,), 0.3, 1.75)
    w_proj = gaussian(key_of[14], (FF, D), FF ** -0.5, 0.09375)
    b_proj = gaussian(key_of[15], (D,), 0.3, 1.75)
    prefix_embed = gaussian(key_of[16], (TASKS, PREFIX, D), 1.0, 6.0, ((0, 4),))
    reparam_in = gaussian(key_of[17], (TASKS, D, RANK), D ** -0.5, 0.1875, ((0, 4),))
    reparam_in_bias = gaussian(key_of[18], (TASKS, RANK), 0.5, 3.0, ((0, 4),))
    reparam_out = gaussian(key_of[19], (TASKS, RANK, 2 * D), RANK ** -0.5, 0.25, ((0, 4),))
    reparam_out_bias = gaussian(key_of[20], (TASKS, 2 * D), 0.5, 3.0, ((0, 4),))
    return {"tokens": tokens, "cotangent": cotangent, "segment_ids": segment_ids, "task_ids": task_ids, "ln1_gain": ln1_gain, "ln1_bias": ln1_bias, "w_qkv": w_qkv, "b_qkv": b_qkv, "w_attn_out": w_attn_out, "b_attn_out": b_attn_out, "ln2_gain": ln2_gain, "ln2_bias": ln2_bias, "w_fc": w_fc, "b_fc": b_fc, "w_proj": w_proj, "b_proj": b_proj, "prefix_embed": prefix_embed, "reparam_in": reparam_in, "reparam_in_bias": reparam_in_bias, "reparam_out": reparam_out, "reparam_out_bias": reparam_out_bias}


epsilon = 1e-05
highest = lax.Precision.HIGHEST
negative = -1e+30

@jax.custom_vjp
def low(v):
    return lax.optimization_barrier(v.astype(jnp.bfloat16)).astype(jnp.float32)

@jax.custom_vjp
def low_back(v):
    return v

def low_keep(v):
    return (low(v), None)

def low_pass(kept, grad):
    return (grad,)

def back_keep(v):
    return (v, None)

def back_low(kept, grad):
    return (low(grad),)
low.defvjp(low_keep, low_pass)
low_back.defvjp(back_keep, back_low)

def layer_norm(hidden, gain, shift):
    center = lax.optimization_barrier(jnp.mean(hidden, axis=-1, keepdims=True))
    centred = hidden - center
    spread = lax.optimization_barrier(jnp.mean(centred * centred, axis=-1, keepdims=True))
    return centred * lax.rsqrt(spread + epsilon) * gain + shift

def gelu_tanh(values):
    return 0.5 * values * (1.0 + jnp.tanh(0.7978845608028654 * (values + 0.044715 * values * values * values)))

def prefix_forward(embed, weight_in, bias_in, weight_out, bias_out):
    pre_hidden = low_back(jnp.einsum('tpd,tdr->tpr', low(embed), weight_in, precision=highest) + bias_in[:, None, :])
    hidden = jnp.tanh(pre_hidden)
    return low_back(low(jnp.einsum('tpr,tre->tpe', low(hidden), weight_out, precision=highest) + bias_out[:, None, :]))

def block_row(row, segments, row_tasks, states, weights):
    gain_one, shift_one, w_qkv, b_qkv, w_attn, b_attn, gain_two, shift_two, w_fc, b_fc, w_proj, b_proj = weights
    seq_len, width = row.shape
    head_dim = width // HEADS
    scale = head_dim ** (-0.5)
    normed = low(layer_norm(row, gain_one, shift_one))
    mixed = jnp.dot(normed, w_qkv, precision=highest) + b_qkv
    queries = low_back(low(mixed[:, :width])).reshape(seq_len, HEADS, head_dim)
    keys_all = low_back(low(mixed[:, width:2 * width])).reshape(seq_len, HEADS, head_dim)
    values_all = low_back(low(mixed[:, 2 * width:])).reshape(seq_len, HEADS, head_dim)
    prefix_keys = states[:, :, :width].reshape(-1, HEADS, head_dim)
    prefix_values = states[:, :, width:].reshape(-1, HEADS, head_dim)
    own_scores = jnp.einsum('qhd,khd->hqk', queries, keys_all, precision=highest) * scale
    prefix_scores = jnp.einsum('qhd,khd->hqk', queries, prefix_keys, precision=highest) * scale
    scores = low_back(jnp.concatenate([own_scores, prefix_scores], axis=2))
    position = jnp.arange(seq_len)
    token_task = row_tasks[segments]
    own_mask = (segments[:, None] == segments[None, :]) & (position[None, :] <= position[:, None])
    task_mask = jnp.repeat(token_task[:, None] == jnp.arange(TASKS)[None, :], PREFIX, axis=1)
    full_mask = jnp.concatenate([own_mask, task_mask], axis=1)
    scores = jnp.where(full_mask[None], scores, negative)
    row_max = lax.optimization_barrier(jnp.max(scores, axis=2, keepdims=True))
    expd = jnp.exp(scores - row_max)
    probs = low(expd / lax.optimization_barrier(jnp.sum(expd, axis=2, keepdims=True)))
    attended = jnp.einsum('hqk,khd->qhd', probs[:, :, :seq_len], values_all, precision=highest)
    attended = attended + jnp.einsum('hqk,khd->qhd', probs[:, :, seq_len:], prefix_values, precision=highest)
    attended = low_back(low(attended.reshape(seq_len, width)))
    branch = low_back(jnp.dot(attended, w_attn, precision=highest) + b_attn)
    resid = row + branch
    normed_two = low(layer_norm(resid, gain_two, shift_two))
    pre_act = low_back(jnp.dot(normed_two, w_fc, precision=highest) + b_fc)
    activation = low(gelu_tanh(pre_act))
    return resid + jnp.dot(activation, w_proj, precision=highest) + b_proj

def reference(tokens, cotangent, segment_ids, task_ids, ln1_gain, ln1_bias, w_qkv, b_qkv, w_attn_out, b_attn_out, ln2_gain, ln2_bias, w_fc, b_fc, w_proj, b_proj, prefix_embed, reparam_in, reparam_in_bias, reparam_out, reparam_out_bias):
    weights = tuple((item.astype(jnp.float32) for item in (ln1_gain, ln1_bias, w_qkv, b_qkv, w_attn_out, b_attn_out, ln2_gain, ln2_bias, w_fc, b_fc, w_proj, b_proj)))
    rows = tokens.reshape(-1, SEQ, D).astype(jnp.float32)
    segments = segment_ids.reshape(-1, SEQ)
    tasks = task_ids.reshape(-1, SEGS)

    def forward(rows_in, embed, weight_in, bias_in, weight_out, bias_out):
        states = prefix_forward(embed, weight_in, bias_in, weight_out, bias_out)

        @jax.checkpoint
        def single(row, row_segments, row_tasks):
            return block_row(row, row_segments, row_tasks, states, weights)

        def advance(carry, item):
            return (carry, single(item[0], item[1], item[2]))
        _, outputs = lax.scan(advance, jnp.zeros((), jnp.float32), (rows_in, segments, tasks))
        return outputs
    outputs, pullback = jax.vjp(forward, rows, prefix_embed.astype(jnp.float32), reparam_in.astype(jnp.float32), reparam_in_bias.astype(jnp.float32), reparam_out.astype(jnp.float32), reparam_out_bias.astype(jnp.float32))
    grads = pullback(cotangent.reshape(-1, SEQ, D).astype(jnp.float32))
    block_out = outputs.reshape(tokens.shape).astype(jnp.bfloat16)
    input_grad = grads[0].reshape(tokens.shape).astype(jnp.bfloat16)
    return (block_out, input_grad, grads[1], grads[2], grads[3], grads[4], grads[5])
```

```python
import functools

import jax
import jax.numpy as jnp
from jax import lax
from jax.experimental import pallas as pl
from jax.experimental.pallas import tpu as pltpu
from jax.sharding import PartitionSpec as P

bf16 = jnp.bfloat16
f32 = jnp.float32

HEADS = 16
HEAD_DIM = 64
GROUP = 4
LANES = GROUP * HEAD_DIM
QB = 64
MOST = 128
WIN = MOST + QB
PAD = 16
EPSILON = 1e-05
NEGATIVE = -1e30
LOG2E = 1.4426950408889634
LN2 = 0.6931471805599453
GELU_A = 0.7978845608028654
GELU_B = 0.044715
MIB = 1 << 20
MESH = pl.DeviceIdType.MESH


def dot_nn(left, right):
    return jnp.dot(left, right, preferred_element_type=f32)


def dot_nt(left, right):
    return lax.dot_general(
        left, right, (((1,), (1,)), ((), ())), preferred_element_type=f32
    )


def dot_tn(left, right):
    return lax.dot_general(
        left, right, (((0,), (0,)), ((), ())), preferred_element_type=f32
    )


def row_vector(ref, part=slice(None)):
    return ref[part].astype(f32)[None, :]


def normalise(hidden):
    centred = hidden - jnp.mean(hidden, axis=1, keepdims=True)
    spread = jnp.mean(centred * centred, axis=1, keepdims=True)
    inverse = lax.rsqrt(spread + EPSILON)
    return centred * inverse, inverse


def norm_backward(grad, gain, unit, inverse):
    scaled = grad * gain
    mean_one = jnp.mean(scaled, axis=1, keepdims=True)
    mean_two = jnp.mean(scaled * unit, axis=1, keepdims=True)
    return inverse * (scaled - mean_one - unit * mean_two)


def gelu_both(value, grad):
    square = value * value
    half = 0.5 + 0.5 * jnp.tanh(value * (GELU_A + (GELU_A * GELU_B) * square))
    act = value * half
    slope = half + (act * (2 * GELU_A + (6 * GELU_A * GELU_B) * square)) * (1.0 - half)
    return act.astype(bf16), (grad * slope).astype(bf16)


def barrier_with(peers):
    barrier = pltpu.get_barrier_semaphore()
    for peer in peers:
        pl.semaphore_signal(barrier, inc=1, device_id=peer, device_id_type=MESH)
    return barrier


def qkv_kernel(
    tasks,
    tok_ref,
    gain_ref,
    shift_ref,
    w_ref,
    b_ref,
    embed_ref,
    win_hbm,
    bin_ref,
    wout_hbm,
    bout_ref,
    mixed_ref,
    hidden_ref,
    states_ref,
    win,
    wout,
    padded,
    own,
    gathered,
    load_sem,
    send_sem,
    recv_sem,
):
    step = pl.program_id(0)
    steps = pl.num_programs(0)
    row_axis = lax.axis_index("batch")
    me = lax.axis_index("task")
    peers = [(row_axis, lax.rem(me + k, tasks)) for k in range(1, tasks)]

    def load(index):
        source, target = ((win_hbm, win), (wout_hbm, wout))[index]
        return pltpu.make_async_copy(source.at[0], target, load_sem.at[index])

    def send(k):
        return pltpu.make_async_remote_copy(
            src_ref=own,
            dst_ref=gathered.at[me],
            send_sem=send_sem.at[k - 1],
            recv_sem=recv_sem.at[k - 1],
            device_id=peers[k - 1],
            device_id_type=MESH,
        )

    @pl.when(step == 0)
    def _():
        load(0).start()
        load(1).start()
        barrier_with(peers)

    @pl.when(step == 1)
    def _():
        load(0).wait()
        load(1).wait()
        padded[...] = jnp.zeros(padded.shape, f32)
        padded[: embed_ref.shape[1], :] = embed_ref[0].astype(f32)
        pre = dot_nn(padded[...].astype(bf16), win[...]) + bin_ref[...].astype(f32)
        hidden = jnp.tanh(pre)
        hidden_ref[...] = hidden
        states = dot_nn(hidden.astype(bf16), wout[...]) + bout_ref[...].astype(f32)
        states = states.astype(bf16)
        own[...] = states
        gathered[me] = states
        pl.semaphore_wait(pltpu.get_barrier_semaphore(), tasks - 1)
        for k in range(1, tasks):
            send(k).start()

    normed, _ = normalise(tok_ref[...].astype(f32))
    normed = (normed * row_vector(gain_ref) + row_vector(shift_ref)).astype(bf16)
    width = tok_ref.shape[1]
    mixed = dot_nn(normed, w_ref[...]) + row_vector(b_ref)
    mixed_ref[:, :width] = (mixed[:, :width] * (HEAD_DIM ** (-0.5) * LOG2E)).astype(bf16)
    mixed_ref[:, width:] = mixed[:, width:].astype(bf16)

    @pl.when(step == steps - 1)
    def _():
        for k in range(1, tasks):
            send(k).wait()
        states_ref[...] = gathered[...].reshape(states_ref.shape)


def qkv_call(tasks, tokens, gain, shift, w_qkv, b_qkv, embed, w_in, b_in, w_out, b_out):
    micro, rows, seq, width = tokens.shape
    tile = 512
    per_row = seq // tile
    rank = w_in.shape[2]
    whole1 = lambda x: pl.BlockSpec(x.shape, lambda i: (0,) * x.ndim)
    once = lambda x: pl.BlockSpec(
        x.shape, lambda i: (0,) * x.ndim, pipeline_mode=pl.Buffered(1)
    )
    return pl.pallas_call(
        functools.partial(qkv_kernel, tasks),
        grid=(micro * rows * per_row,),
        in_specs=[
            pl.BlockSpec(
                (None, None, tile, width),
                lambda i: (i // (rows * per_row), (i // per_row) % rows, i % per_row, 0),
            ),
            whole1(gain),
            whole1(shift),
            once(w_qkv),
            whole1(b_qkv),
            whole1(embed),
            pl.BlockSpec(memory_space=pl.ANY),
            whole1(b_in),
            pl.BlockSpec(memory_space=pl.ANY),
            whole1(b_out),
        ],
        out_specs=[
            pl.BlockSpec((tile, 3 * width), lambda i: (i, 0)),
            pl.BlockSpec((PAD, rank), lambda i: (0, 0)),
            pl.BlockSpec((tasks * PAD, 2 * width), lambda i: (0, 0)),
        ],
        out_shape=[
            jax.ShapeDtypeStruct((micro * rows * seq, 3 * width), bf16),
            jax.ShapeDtypeStruct((PAD, rank), f32),
            jax.ShapeDtypeStruct((tasks * PAD, 2 * width), bf16),
        ],
        scratch_shapes=[
            pltpu.VMEM(w_in.shape[1:], bf16),
            pltpu.VMEM(w_out.shape[1:], bf16),
            pltpu.VMEM((PAD, width), f32),
            pltpu.VMEM((PAD, 2 * width), bf16),
            pltpu.VMEM((tasks, PAD, 2 * width), bf16),
            pltpu.SemaphoreType.DMA((2,)),
            pltpu.SemaphoreType.DMA((tasks - 1,)),
            pltpu.SemaphoreType.DMA((tasks - 1,)),
        ],
        compiler_params=pltpu.CompilerParams(
            collective_id=0, has_side_effects=True, vmem_limit_bytes=40 * MIB
        ),
        name="norm_qkv",
    )(tokens, gain, shift, w_qkv, b_qkv, embed, w_in, b_in, w_out, b_out)


def stack_heads(block):
    lane = lax.broadcasted_iota(jnp.int32, (QB, 128), 1)
    zero = jnp.zeros((QB, 128), block.dtype)
    rows = []
    for h in range(GROUP):
        part = jnp.where((lane < HEAD_DIM) == (h % 2 == 0), block[:, (h // 2) * 128 :][:, :128], zero)
        rows.append(jnp.concatenate([part, zero] if h < 2 else [zero, part], axis=1))
    return jnp.concatenate(rows, axis=0)


def pick_heads(stacked):
    lane = lax.broadcasted_iota(jnp.int32, (QB, 128), 1)
    low = jnp.where(lane < HEAD_DIM, stacked[:QB, :128], stacked[QB : 2 * QB, :128])
    high = jnp.where(lane < HEAD_DIM, stacked[2 * QB : 3 * QB, 128:], stacked[3 * QB :, 128:])
    return jnp.concatenate([low, high], axis=1)


def fill_mask(seg_ref, task_ref, micro, prefix, bias, by_key):
    segments = seg_ref[...]
    seq = segments.shape[1]
    token_task = jnp.zeros(segments.shape, jnp.int32)
    for s in range(task_ref.shape[-1]):
        token_task = jnp.where(segments == s, task_ref[micro, 0, s], token_task)
    segments = segments.astype(f32)
    for c in range(0, seq, 128):
        by_key[c : c + 128, :] = jnp.broadcast_to(segments[:, c : c + 128], (128, 128)).T
    for b in range(seq // QB):
        start = max(b * QB - MOST, 0)

        def twice(x):
            part = x[:, b * QB : (b + 1) * QB]
            return jnp.concatenate([part, part], axis=1)

        key_pos = start + lax.broadcasted_iota(jnp.int32, (WIN, 128), 0)
        query_pos = b * QB + (lax.broadcasted_iota(jnp.int32, (WIN, 128), 1) & (QB - 1))
        own = (by_key[start : start + WIN, :] == twice(segments)) & (key_pos <= query_pos)
        bias[b, :WIN, :] = jnp.where(own, 0.0, NEGATIVE)
        index = lax.broadcasted_iota(jnp.int32, (bias.shape[1] - WIN, 128), 0)
        fits = (lax.shift_right_logical(index, 4) == twice(token_task)) & (
            (index & (PAD - 1)) < prefix
        )
        bias[b, WIN:, :] = jnp.where(fits, 0.0, NEGATIVE)


def attention_kernel(
    prefix, task_ref, seg_ref, q_ref, k_ref, v_ref, pk_ref, pv_ref, out_ref, probs_ref, bias, by_key
):
    micro = pl.program_id(0)

    @pl.when(pl.program_id(1) == 0)
    def _():
        fill_mask(seg_ref, task_ref, micro, prefix, bias, by_key)

    for b in range(q_ref.shape[0] // QB):
        rows = slice(b * QB, (b + 1) * QB)
        start = max(b * QB - MOST, 0)
        window = slice(start, start + WIN)
        keys = jnp.concatenate([k_ref[window, :], pk_ref[...]], axis=0)
        values = jnp.concatenate([v_ref[window, :], pv_ref[...]], axis=0)
        scores = dot_nt(keys, stack_heads(q_ref[rows, :]))
        scores = scores + jnp.concatenate([bias[b], bias[b]], axis=1)
        powers = jnp.exp2(scores - jnp.max(scores, axis=0, keepdims=True))
        total = jnp.sum(powers, axis=0, keepdims=True)
        probs = (powers * (1.0 / total)).astype(bf16)
        probs_ref[b] = probs
        out_ref[rows, :] = pick_heads(dot_tn(probs, values)).astype(bf16)


def attention_call(mixed, segments, tasks, states, prefix):
    micro, _, seq = segments.shape
    width = mixed.shape[1] // 3
    groups = width // LANES
    blocks = seq // QB
    keys = WIN + states.shape[0]
    part = lambda offset: pl.BlockSpec((seq, LANES), lambda r, g: (r, offset + g))
    piece = lambda offset: pl.BlockSpec((states.shape[0], LANES), lambda r, g: (0, offset + g))
    return pl.pallas_call(
        functools.partial(attention_kernel, prefix),
        grid=(micro, groups),
        in_specs=[
            pl.BlockSpec(memory_space=pltpu.SMEM),
            pl.BlockSpec((None, 1, seq), lambda r, g: (r, 0, 0)),
            part(0),
            part(groups),
            part(2 * groups),
            piece(0),
            piece(groups),
        ],
        out_specs=[
            part(0),
            pl.BlockSpec((None, None, blocks, keys, LANES), lambda r, g: (r, g, 0, 0, 0)),
        ],
        out_shape=[
            jax.ShapeDtypeStruct((micro * seq, width), bf16),
            jax.ShapeDtypeStruct((micro, groups, blocks, keys, LANES), bf16),
        ],
        scratch_shapes=[pltpu.VMEM((blocks, keys, 128), f32), pltpu.VMEM((seq, 128), f32)],
        compiler_params=pltpu.CompilerParams(vmem_limit_bytes=24 * MIB),
        name="attention",
    )(tasks, segments, mixed, mixed, mixed, states, states)


def mlp_kernel(
    att_ref,
    tok_ref,
    cot_ref,
    wa_ref,
    ba_ref,
    gain_ref,
    shift_ref,
    wf_ref,
    bf_ref,
    wp_ref,
    bp_ref,
    out_ref,
    gres_ref,
    gatt_ref,
    act_all,
    gpre_all,
):
    w_attn = wa_ref[...]
    gain = row_vector(gain_ref)
    resid = tok_ref[...].astype(f32) + dot_nn(att_ref[...], w_attn) + row_vector(ba_ref)
    unit, inverse = normalise(resid)
    normed = (unit * gain + row_vector(shift_ref)).astype(bf16)
    grad_out = cot_ref[...]
    chunk = 512
    for start in range(0, wf_ref.shape[1], chunk):
        part = slice(start, start + chunk)
        pre = dot_nn(normed, wf_ref[:, part]) + row_vector(bf_ref, part)
        act, gpre = gelu_both(pre, dot_nt(grad_out, wp_ref[part, :]))
        act_all[:, part] = act
        gpre_all[:, part] = gpre
    out = resid + dot_nn(act_all[...], wp_ref[...]) + row_vector(bp_ref)
    out_ref[...] = out.astype(bf16)
    grad_normed = dot_nt(gpre_all[...], wf_ref[...])
    grad_resid = grad_out.astype(f32) + norm_backward(grad_normed, gain, unit, inverse)
    gres_ref[...] = grad_resid
    gatt_ref[...] = dot_nt(grad_resid.astype(bf16), w_attn).astype(bf16)


def mlp_call(attended, tokens, cotangent, w_attn, b_attn, gain, shift, w_fc, b_fc, w_proj, b_proj):
    micro, rows, seq, width = tokens.shape
    tile = 512
    per_row = seq // tile
    flat = pl.BlockSpec((tile, width), lambda i: (i, 0))
    deep = pl.BlockSpec(
        (None, None, tile, width),
        lambda i: (i // (rows * per_row), (i // per_row) % rows, i % per_row, 0),
    )
    once = lambda x: pl.BlockSpec(
        x.shape, lambda i: (0,) * x.ndim, pipeline_mode=pl.Buffered(1)
    )
    weights = (w_attn, b_attn, gain, shift, w_fc, b_fc, w_proj, b_proj)
    count = micro * rows * seq
    return pl.pallas_call(
        mlp_kernel,
        grid=(count // tile,),
        in_specs=[flat, deep, deep] + [once(x) for x in weights],
        out_specs=[deep, flat, flat],
        out_shape=[
            jax.ShapeDtypeStruct(tokens.shape, bf16),
            jax.ShapeDtypeStruct((count, width), f32),
            jax.ShapeDtypeStruct((count, width), bf16),
        ],
        scratch_shapes=[pltpu.VMEM((tile, w_fc.shape[1]), bf16)] * 2,
        compiler_params=pltpu.CompilerParams(vmem_limit_bytes=60 * MIB),
        name="feed_forward",
    )(attended, tokens, cotangent, *weights)


def attention_grad_kernel(
    q_ref,
    k_ref,
    v_ref,
    pk_ref,
    pv_ref,
    probs_ref,
    g_ref,
    dq_ref,
    dk_ref,
    dv_ref,
    dpk_ref,
    dpv_ref,
    key_sum,
    value_sum,
    prefix_key_sum,
    prefix_value_sum,
):
    for b in range(q_ref.shape[0] // QB):
        rows = slice(b * QB, (b + 1) * QB)
        start = max(b * QB - MOST, 0)
        window = slice(start, start + WIN)
        keys = jnp.concatenate([k_ref[window, :], pk_ref[...]], axis=0)
        values = jnp.concatenate([v_ref[window, :], pv_ref[...]], axis=0)
        queries = stack_heads(q_ref[rows, :])
        grads = stack_heads(g_ref[rows, :])
        probs = probs_ref[b]
        weight = probs.astype(f32)
        product = weight * dot_nt(values, grads)
        delta = jnp.sum(product, axis=0, keepdims=True)
        score_grad = (product - weight * delta).astype(bf16)
        dv = dot_nn(probs, grads)
        dk = dot_nn(score_grad, queries)
        dq = pick_heads(dot_tn(score_grad, keys))
        dq_ref[rows, :] = (dq * HEAD_DIM ** (-0.5)).astype(bf16)
        old = 0 if b == 0 else min(WIN, b * QB - start) if start else WIN
        for total, fresh in ((key_sum, dk), (value_sum, dv)):
            if old:
                total[start : start + old, :] += fresh[:old]
            if old < WIN:
                total[start + old : start + WIN, :] = fresh[old:WIN]
        if b == 0:
            prefix_key_sum[...] = dk[WIN:]
            prefix_value_sum[...] = dv[WIN:]
        else:
            prefix_key_sum[...] += dk[WIN:]
            prefix_value_sum[...] += dv[WIN:]
    dk_ref[...] = (key_sum[...] * LN2).astype(bf16)
    dv_ref[...] = value_sum[...].astype(bf16)

    @pl.when(pl.program_id(1) == 0)
    def _():
        dpk_ref[...] = prefix_key_sum[...] * LN2
        dpv_ref[...] = prefix_value_sum[...]

    @pl.when(pl.program_id(1) != 0)
    def _():
        dpk_ref[...] += prefix_key_sum[...] * LN2
        dpv_ref[...] += prefix_value_sum[...]


def attention_grad_call(mixed, states, probs, grad_attended):
    micro, groups, blocks, keys, _ = probs.shape
    seq = blocks * QB
    width = grad_attended.shape[1]
    prefix_rows = states.shape[0]
    part = lambda offset: pl.BlockSpec((seq, LANES), lambda g, r: (r, offset + g))
    piece = lambda offset: pl.BlockSpec((prefix_rows, LANES), lambda g, r: (0, offset + g))
    return pl.pallas_call(
        attention_grad_kernel,
        grid=(groups, micro),
        in_specs=[
            part(0),
            part(groups),
            part(2 * groups),
            piece(0),
            piece(groups),
            pl.BlockSpec((None, None, blocks, keys, LANES), lambda g, r: (r, g, 0, 0, 0)),
            part(0),
        ],
        out_specs=[part(0)] * 3 + [piece(0)] * 2,
        out_shape=[jax.ShapeDtypeStruct((micro * seq, width), bf16)] * 3
        + [jax.ShapeDtypeStruct((prefix_rows, width), f32)] * 2,
        scratch_shapes=[pltpu.VMEM((seq, LANES), f32)] * 2
        + [pltpu.VMEM((prefix_rows, LANES), f32)] * 2,
        compiler_params=pltpu.CompilerParams(vmem_limit_bytes=24 * MIB),
        name="attention_grad",
    )(mixed, mixed, mixed, states, states, probs, grad_attended)


def input_grad_tile(dq_ref, dk_ref, dv_ref, tok_ref, gres_ref, gain_ref, w_ref):
    width = dq_ref.shape[1]
    grad = dot_nt(dq_ref[...], w_ref[:, :width])
    grad = grad + dot_nt(dk_ref[...], w_ref[:, width : 2 * width])
    grad = grad + dot_nt(dv_ref[...], w_ref[:, 2 * width :])
    unit, inverse = normalise(tok_ref[...].astype(f32))
    back = norm_backward(grad, row_vector(gain_ref), unit, inverse)
    return (gres_ref[...] + back).astype(bf16)


def sum_kernel(
    tasks,
    shards,
    dq_ref,
    dk_ref,
    dv_ref,
    tok_ref,
    gres_ref,
    gain_ref,
    w_ref,
    dpk_ref,
    dpv_ref,
    grad_ref,
    summed_ref,
    send_a,
    recv_a,
    send_b,
    recv_b,
    gathered,
    sems,
    sems_b,
):
    step = pl.program_id(0)
    shard = lax.axis_index("batch")
    task = lax.axis_index("task")
    task_peers = [(shard, lax.rem(task + k, tasks)) for k in range(1, tasks)]
    shard_peers = [(lax.rem(shard + k, shards), task) for k in range(1, shards)]
    width = dpk_ref.shape[1]
    lanes = send_b.shape[2]

    def to_task(k):
        return pltpu.make_async_remote_copy(
            src_ref=send_a.at[lax.rem(task + k, tasks)],
            dst_ref=recv_a.at[k - 1],
            send_sem=sems.at[0, k - 1],
            recv_sem=sems.at[1, k - 1],
            device_id=task_peers[k - 1],
            device_id_type=MESH,
        )

    def to_shard(k):
        return pltpu.make_async_remote_copy(
            src_ref=send_b.at[lax.rem(shard + k, shards)],
            dst_ref=recv_b.at[k - 1],
            send_sem=sems_b.at[0, k - 1],
            recv_sem=sems_b.at[1, k - 1],
            device_id=shard_peers[k - 1],
            device_id_type=MESH,
        )

    def back_to_shard(k):
        return pltpu.make_async_remote_copy(
            src_ref=gathered.at[shard],
            dst_ref=gathered.at[shard],
            send_sem=sems_b.at[2, k - 1],
            recv_sem=sems_b.at[3, k - 1],
            device_id=shard_peers[k - 1],
            device_id_type=MESH,
        )

    @pl.when(step == 0)
    def _():
        barrier_with(task_peers + shard_peers)
        for t in range(tasks):
            part = slice(t * PAD, (t + 1) * PAD)
            send_a[t, :, :width] = dpk_ref[part, :].astype(bf16)
            send_a[t, :, width:] = dpv_ref[part, :].astype(bf16)

    @pl.when(step == 1)
    def _():
        pl.semaphore_wait(pltpu.get_barrier_semaphore(), tasks - 1 + shards - 1)
        for k in range(1, tasks):
            to_task(k).start()

    @pl.when(step == 2)
    def _():
        for k in range(1, tasks):
            to_task(k).wait()
        total = send_a[task].astype(f32)
        for k in range(1, tasks):
            total = total + recv_a[k - 1].astype(f32)
        total = total.astype(bf16)
        for c in range(shards):
            send_b[c] = total[:, c * lanes : (c + 1) * lanes]
        for k in range(1, shards):
            to_shard(k).start()

    @pl.when(step == 3)
    def _():
        for k in range(1, shards):
            to_shard(k).wait()
        total = send_b[shard].astype(f32)
        for k in range(1, shards):
            total = total + recv_b[k - 1].astype(f32)
        gathered[shard] = total.astype(bf16)
        for k in range(1, shards):
            back_to_shard(k).start()

    grad_ref[...] = input_grad_tile(
        dq_ref, dk_ref, dv_ref, tok_ref, gres_ref, gain_ref, w_ref
    )

    @pl.when(step == 3)
    def _():
        for k in range(1, shards):
            back_to_shard(k).wait()
        for c in range(shards):
            summed_ref[:, c * lanes : (c + 1) * lanes] = gathered[c]


def sum_call(tasks, shards, dq, dk, dv, tokens, grad_resid, gain, w_qkv, dpk, dpv):
    seq, width = tokens.shape[2:]
    tile = seq // 4
    flat = pl.BlockSpec((tile, width), lambda i: (i, 0))
    once = lambda x: pl.BlockSpec(
        x.shape, lambda i: (0,) * x.ndim, pipeline_mode=pl.Buffered(1)
    )
    lanes = 2 * width // shards
    return pl.pallas_call(
        functools.partial(sum_kernel, tasks, shards),
        grid=(4,),
        in_specs=[flat, flat, flat]
        + [pl.BlockSpec((None, None, tile, width), lambda i: (0, 0, i, 0)), flat]
        + [once(x) for x in (gain, w_qkv, dpk, dpv)],
        out_specs=[flat, pl.BlockSpec((PAD, 2 * width), lambda i: (0, 0))],
        out_shape=[
            jax.ShapeDtypeStruct((seq, width), bf16),
            jax.ShapeDtypeStruct((PAD, 2 * width), bf16),
        ],
        scratch_shapes=[
            pltpu.VMEM((tasks, PAD, 2 * width), bf16),
            pltpu.VMEM((tasks - 1, PAD, 2 * width), bf16),
            pltpu.VMEM((shards, PAD, lanes), bf16),
            pltpu.VMEM((shards - 1, PAD, lanes), bf16),
            pltpu.VMEM((shards, PAD, lanes), bf16),
            pltpu.SemaphoreType.DMA((2, tasks - 1)),
            pltpu.SemaphoreType.DMA((4, shards - 1)),
        ],
        compiler_params=pltpu.CompilerParams(
            collective_id=1, has_side_effects=True, vmem_limit_bytes=32 * MIB
        ),
        name="grad_first_sum",
    )(dq, dk, dv, tokens, grad_resid, gain, w_qkv, dpk, dpv)


def last_kernel(
    dq_ref,
    dk_ref,
    dv_ref,
    tok_ref,
    gres_ref,
    gain_ref,
    w_ref,
    first_hbm,
    summed_ref,
    hidden_ref,
    embed_ref,
    win_ref,
    wout_ref,
    out_hbm,
    gembed_ref,
    gin_hbm,
    gbin_ref,
    gout_hbm,
    gbout_ref,
    tile_out,
    padded,
    gin,
    gout,
    sems,
):
    step = pl.program_id(0)
    steps = pl.num_programs(0)
    tile = dq_ref.shape[0]

    def pass_on():
        return pltpu.make_async_copy(first_hbm, out_hbm.at[0, 0], sems.at[0])

    def put_in():
        return pltpu.make_async_copy(gin, gin_hbm.at[0], sems.at[1])

    def put_out():
        return pltpu.make_async_copy(gout, gout_hbm.at[0], sems.at[2])

    def put_tile(index):
        return pltpu.make_async_copy(
            tile_out.at[index],
            out_hbm.at[out_hbm.shape[0] - 1, 0, pl.ds(index * tile, tile), :],
            sems.at[3 + index],
        )

    @pl.when(step == 0)
    def _():
        pass_on().start()
        summed = summed_ref[...]
        hidden = hidden_ref[...]
        gout[...] = dot_tn(hidden.astype(bf16), summed)
        put_out().start()
        gbout_ref[...] = jnp.sum(summed.astype(f32), axis=0, keepdims=True)
        grad_hidden = dot_nt(summed, wout_ref[0])
        grad_pre = (grad_hidden * (1.0 - hidden * hidden)).astype(bf16)
        padded[...] = jnp.zeros(padded.shape, f32)
        padded[: embed_ref.shape[1], :] = embed_ref[0].astype(f32)
        gin[...] = dot_tn(padded[...].astype(bf16), grad_pre)
        put_in().start()
        gbin_ref[...] = jnp.sum(grad_pre.astype(f32), axis=0, keepdims=True)
        gembed_ref[0] = dot_nt(grad_pre, win_ref[0])[: embed_ref.shape[1], :]

    result = input_grad_tile(dq_ref, dk_ref, dv_ref, tok_ref, gres_ref, gain_ref, w_ref)
    for index in range(tile_out.shape[0]):

        @pl.when(step == index)
        def _():
            tile_out[index] = result
            put_tile(index).start()

    @pl.when(step == steps - 1)
    def _():
        pass_on().wait()
        put_in().wait()
        put_out().wait()
        for index in range(tile_out.shape[0]):
            put_tile(index).wait()


def last_call(dq, dk, dv, tokens, grad_resid, gain, w_qkv, first, summed, hidden, embed, w_in, w_out):
    micro, _, seq, width = tokens.shape
    tile = 512
    tiles = seq // tile
    flat = pl.BlockSpec((tile, width), lambda i: ((micro - 1) * tiles + i, 0))
    anywhere = pl.BlockSpec(memory_space=pl.ANY)
    once = lambda x: pl.BlockSpec(
        x.shape, lambda i: (0,) * x.ndim, pipeline_mode=pl.Buffered(1)
    )
    whole = lambda shape: pl.BlockSpec(shape, lambda i: (0,) * len(shape))
    rank = w_in.shape[2]
    return pl.pallas_call(
        last_kernel,
        grid=(tiles,),
        in_specs=[flat, flat, flat]
        + [pl.BlockSpec((None, None, tile, width), lambda i: (micro - 1, 0, i, 0)), flat]
        + [once(gain), once(w_qkv), anywhere]
        + [once(x) for x in (summed, hidden, embed, w_in, w_out)],
        out_specs=[
            anywhere,
            whole(embed.shape),
            anywhere,
            whole((1, rank)),
            anywhere,
            whole((1, 2 * width)),
        ],
        out_shape=[
            jax.ShapeDtypeStruct(tokens.shape, bf16),
            jax.ShapeDtypeStruct(embed.shape, f32),
            jax.ShapeDtypeStruct(w_in.shape, f32),
            jax.ShapeDtypeStruct((1, rank), f32),
            jax.ShapeDtypeStruct(w_out.shape, f32),
            jax.ShapeDtypeStruct((1, 2 * width), f32),
        ],
        scratch_shapes=[
            pltpu.VMEM((tiles, tile, width), bf16),
            pltpu.VMEM((PAD, width), f32),
            pltpu.VMEM(w_in.shape[1:], f32),
            pltpu.VMEM(w_out.shape[1:], f32),
            pltpu.SemaphoreType.DMA((3 + tiles,)),
        ],
        compiler_params=pltpu.CompilerParams(vmem_limit_bytes=48 * MIB),
        name="grad_last",
    )(dq, dk, dv, tokens, grad_resid, gain, w_qkv, first, summed, hidden, embed, w_in, w_out)


def on_device(
    tasks,
    shards,
    tokens,
    cotangent,
    segment_ids,
    task_ids,
    ln1_gain,
    ln1_bias,
    w_qkv,
    b_qkv,
    w_attn_out,
    b_attn_out,
    ln2_gain,
    ln2_bias,
    w_fc,
    b_fc,
    w_proj,
    b_proj,
    prefix_embed,
    reparam_in,
    reparam_in_bias,
    reparam_out,
    reparam_out_bias,
):
    mixed, hidden, states = qkv_call(
        tasks,
        tokens,
        ln1_gain,
        ln1_bias,
        w_qkv,
        b_qkv,
        prefix_embed,
        reparam_in,
        reparam_in_bias,
        reparam_out,
        reparam_out_bias,
    )
    attended, probs = attention_call(
        mixed, segment_ids, task_ids, states, prefix_embed.shape[1]
    )
    block_out, grad_resid, grad_attended = mlp_call(
        attended,
        tokens,
        cotangent,
        w_attn_out,
        b_attn_out,
        ln2_gain,
        ln2_bias,
        w_fc,
        b_fc,
        w_proj,
        b_proj,
    )
    dq, dk, dv, dpk, dpv = attention_grad_call(mixed, states, probs, grad_attended)
    first, summed = sum_call(
        tasks, shards, dq, dk, dv, tokens, grad_resid, ln1_gain, w_qkv, dpk, dpv
    )
    input_grad, gembed, gin, gbin, gout, gbout = last_call(
        dq,
        dk,
        dv,
        tokens,
        grad_resid,
        ln1_gain,
        w_qkv,
        first,
        summed,
        hidden,
        prefix_embed,
        reparam_in,
        reparam_out,
    )
    return (block_out, input_grad, gembed, gin, gbin, gout, gbout)


def solution(mesh):
    split = ("batch", "task")
    in_specs = (
        (P(None, split, None, None),) * 2
        + (P(None, split, None),) * 2
        + (P(),) * 12
        + (
            P("task", None, None),
            P("task", None, None),
            P("task", None),
            P("task", None, None),
            P("task", None),
        )
    )
    out_specs = (
        P(None, split, None, None),
        P(None, split, None, None),
        P("task", None, None),
        P("task", None, None),
        P("task", None),
        P("task", None, None),
        P("task", None),
    )
    return jax.shard_map(
        functools.partial(on_device, mesh.shape["task"], mesh.shape["batch"]),
        mesh=mesh,
        in_specs=in_specs,
        out_specs=out_specs,
        check_vma=False,
    )
```

```python
import functools

import jax
import jax.numpy as jnp
from jax import lax
from jax.experimental import pallas as pl
from jax.experimental.pallas import tpu as pltpu
from jax.sharding import PartitionSpec as P

bf16 = jnp.bfloat16
f32 = jnp.float32

HEADS = 16
HEAD_DIM = 64
GROUP = 4
LANES = GROUP * HEAD_DIM
QB = 64
MOST = 128
WIN = MOST + QB
PAD = 16
EPSILON = 1e-05
NEGATIVE = -1e30
LOG2E = 1.4426950408889634
LN2 = 0.6931471805599453
GELU_A = 0.7978845608028654
GELU_B = 0.044715
VMEM_LIMIT = 62 << 20
CHUNK = 32
QKV_TILE = 256
FF_CHUNK = 1024
MESH = pl.DeviceIdType.MESH


def dot_nn(left, right):
    return jnp.dot(left, right, preferred_element_type=f32)


def dot_nt(left, right):
    return lax.dot_general(
        left, right, (((1,), (1,)), ((), ())), preferred_element_type=f32
    )


def dot_tn(left, right):
    return lax.dot_general(
        left, right, (((0,), (0,)), ((), ())), preferred_element_type=f32
    )


def row_vector(ref, part=slice(None)):
    return ref[part].astype(f32)[None, :]


def normalise(hidden):
    centred = hidden - jnp.mean(hidden, axis=1, keepdims=True)
    spread = jnp.mean(centred * centred, axis=1, keepdims=True)
    inverse = lax.rsqrt(spread + EPSILON)
    return centred * inverse, inverse


def norm_backward(grad, gain, unit, inverse):
    scaled = grad * gain
    mean_one = jnp.mean(scaled, axis=1, keepdims=True)
    mean_two = jnp.mean(scaled * unit, axis=1, keepdims=True)
    return inverse * (scaled - mean_one - unit * mean_two)


def gelu_both(value, grad):
    square = value * value
    half = 0.5 + 0.5 * jnp.tanh(value * (GELU_A + (GELU_A * GELU_B) * square))
    act = value * half
    slope = half + (act * (2 * GELU_A + (6 * GELU_A * GELU_B) * square)) * (1.0 - half)
    return act.astype(bf16), (grad * slope).astype(bf16)


def barrier_with(peers):
    barrier = pltpu.get_barrier_semaphore()
    for peer in peers:
        pl.semaphore_signal(barrier, inc=1, device_id=peer, device_id_type=MESH)
    return barrier


def qkv_kernel(
    tasks,
    tok_ref,
    gain_ref,
    shift_ref,
    w_hbm,
    b_ref,
    embed_ref,
    win_hbm,
    bin_ref,
    wout_hbm,
    bout_ref,
    *refs,
):
    count = (len(refs) - 13) // 2
    weights_hbm = refs[:count]
    mixed_ref, hidden_ref, states_ref = refs[count : count + 3]
    weights = refs[count + 3 : 2 * count + 3]
    (
        win,
        wout,
        padded,
        own,
        gathered,
        w_ref,
        current,
        load_sem,
        send_sem,
        recv_sem,
    ) = refs[2 * count + 3 :]
    step = pl.program_id(0)
    last = pl.num_programs(0) - 1
    row_axis = lax.axis_index("batch")
    me = lax.axis_index("task")
    peers = [(row_axis, lax.rem(me + k, tasks)) for k in range(1, tasks)]

    width = tok_ref.shape[1]

    copies = [(w_hbm, w_ref), (win_hbm.at[0], win), (wout_hbm.at[0], wout)]
    copies += list(zip(weights_hbm, weights))

    def load(index):
        return pltpu.make_async_copy(*copies[index], load_sem.at[index])

    def send(k):
        return pltpu.make_async_remote_copy(
            src_ref=own,
            dst_ref=gathered.at[me],
            send_sem=send_sem.at[k - 1],
            recv_sem=recv_sem.at[k - 1],
            device_id=peers[k - 1],
            device_id_type=MESH,
        )

    def norm():
        normed, _ = normalise(tok_ref[...].astype(f32))
        return (normed * row_vector(gain_ref) + row_vector(shift_ref)).astype(bf16)

    @pl.when(step == 0)
    def _():
        load(0).start()
        barrier_with(peers)
        current[...] = norm()
        load(0).wait()
        for index in range(1, len(copies)):
            load(index).start()

    @pl.when(step == 2)
    def _():
        load(1).wait()
        load(2).wait()
        padded[...] = jnp.zeros(padded.shape, f32)
        padded[: embed_ref.shape[1], :] = embed_ref[0].astype(f32)
        pre = dot_nn(padded[...].astype(bf16), win[...]) + bin_ref[...].astype(f32)
        hidden = jnp.tanh(pre)
        hidden_ref[...] = hidden
        states = dot_nn(hidden.astype(bf16), wout[...]) + bout_ref[...].astype(f32)
        states = states.astype(bf16)
        own[...] = states
        gathered[me] = states
        pl.semaphore_wait(pltpu.get_barrier_semaphore(), tasks - 1)
        for k in range(1, tasks):
            send(k).start()

    @pl.when(step > 0)
    def _():
        mixed = dot_nn(current[...], w_ref[...]) + row_vector(b_ref)
        following = norm()
        mixed_ref[:, :width] = (mixed[:, :width] * (HEAD_DIM ** (-0.5) * LOG2E)).astype(bf16)
        mixed_ref[:, width:] = mixed[:, width:].astype(bf16)
        current[...] = following

    @pl.when(step == last)
    def _():
        for k in range(1, tasks):
            send(k).wait()
        states_ref[...] = gathered[...].reshape(states_ref.shape)
        for index in range(3, len(copies)):
            load(index).wait()


def qkv_call(tasks, tokens, gain, shift, w_qkv, b_qkv, embed, w_in, b_in, w_out, b_out, keep):
    micro, rows, seq, width = tokens.shape
    tile = QKV_TILE
    per_row = seq // tile
    rank = w_in.shape[2]
    whole1 = lambda x: pl.BlockSpec(x.shape, lambda i: (0,) * x.ndim)
    tiles = micro * rows * per_row
    ahead = lambda i: jnp.minimum(i, tiles - 1)
    return pl.pallas_call(
        functools.partial(qkv_kernel, tasks),
        grid=(tiles + 1,),
        in_specs=[
            pl.BlockSpec(
                (None, None, tile, width),
                lambda i: (
                    ahead(i) // (rows * per_row),
                    lax.rem(ahead(i) // per_row, rows),
                    lax.rem(ahead(i), per_row),
                    0,
                ),
            ),
            whole1(gain),
            whole1(shift),
            pl.BlockSpec(memory_space=pl.ANY),
            whole1(b_qkv),
            whole1(embed),
            pl.BlockSpec(memory_space=pl.ANY),
            whole1(b_in),
            pl.BlockSpec(memory_space=pl.ANY),
            whole1(b_out),
        ]
        + [pl.BlockSpec(memory_space=pl.ANY)] * len(keep),
        out_specs=[
            pl.BlockSpec((tile, 3 * width), lambda i: (jnp.maximum(i - 1, 0), 0)),
            pl.BlockSpec((PAD, rank), lambda i: (0, 0)),
            pl.BlockSpec((tasks * PAD, 2 * width), lambda i: (0, 0)),
        ]
        + [pl.BlockSpec(memory_space=pltpu.VMEM)] * len(keep),
        out_shape=[
            jax.ShapeDtypeStruct((micro * rows * seq, 3 * width), bf16),
            jax.ShapeDtypeStruct((PAD, rank), f32),
            jax.ShapeDtypeStruct((tasks * PAD, 2 * width), bf16),
        ]
        + [pltpu.VMEM(x.shape, bf16) for x in keep],
        scratch_shapes=[
            pltpu.VMEM(w_in.shape[1:], bf16),
            pltpu.VMEM(w_out.shape[1:], bf16),
            pltpu.VMEM((PAD, width), f32),
            pltpu.VMEM((PAD, 2 * width), bf16),
            pltpu.VMEM((tasks, PAD, 2 * width), bf16),
            pltpu.VMEM(w_qkv.shape, bf16),
            pltpu.VMEM((tile, width), bf16),
            pltpu.SemaphoreType.DMA((3 + len(keep),)),
            pltpu.SemaphoreType.DMA((tasks - 1,)),
            pltpu.SemaphoreType.DMA((tasks - 1,)),
        ],
        compiler_params=pltpu.CompilerParams(
            collective_id=0, has_side_effects=True, vmem_limit_bytes=VMEM_LIMIT
        ),
        name="norm_qkv",
    )(tokens, gain, shift, w_qkv, b_qkv, embed, w_in, b_in, w_out, b_out, *keep)


def stack_heads(block):
    lane = lax.broadcasted_iota(jnp.int32, (QB, 128), 1)
    zero = jnp.zeros((QB, 128), block.dtype)
    rows = []
    for h in range(GROUP):
        part = jnp.where((lane < HEAD_DIM) == (h % 2 == 0), block[:, (h // 2) * 128 :][:, :128], zero)
        rows.append(jnp.concatenate([part, zero] if h < 2 else [zero, part], axis=1))
    return jnp.concatenate(rows, axis=0)


def pick_heads(stacked):
    lane = lax.broadcasted_iota(jnp.int32, (QB, 128), 1)
    low = jnp.where(lane < HEAD_DIM, stacked[:QB, :128], stacked[QB : 2 * QB, :128])
    high = jnp.where(lane < HEAD_DIM, stacked[2 * QB : 3 * QB, 128:], stacked[3 * QB :, 128:])
    return jnp.concatenate([low, high], axis=1)


def fill_mask(seg_ref, task_ref, micro, prefix, bias, by_key):
    segments = seg_ref[...]
    seq = segments.shape[1]
    token_task = jnp.zeros(segments.shape, jnp.int32)
    for s in range(task_ref.shape[-1]):
        token_task = jnp.where(segments == s, task_ref[micro, 0, s], token_task)
    segments = segments.astype(f32)
    for c in range(0, seq, 128):
        by_key[c : c + 128, :] = jnp.broadcast_to(segments[:, c : c + 128], (128, 128)).T
    for b in range(seq // QB):
        start = max(b * QB - MOST, 0)

        def twice(x):
            part = x[:, b * QB : (b + 1) * QB]
            return jnp.concatenate([part, part], axis=1)

        key_pos = start + lax.broadcasted_iota(jnp.int32, (WIN, 128), 0)
        query_pos = b * QB + (lax.broadcasted_iota(jnp.int32, (WIN, 128), 1) & (QB - 1))
        own = (by_key[start : start + WIN, :] == twice(segments)) & (key_pos <= query_pos)
        bias[b, :WIN, :] = jnp.where(own, 0.0, NEGATIVE)
        index = lax.broadcasted_iota(jnp.int32, (bias.shape[1] - WIN, 128), 0)
        fits = (lax.shift_right_logical(index, 4) == twice(token_task)) & (
            (index & (PAD - 1)) < prefix
        )
        bias[b, WIN:, :] = jnp.where(fits, 0.0, NEGATIVE)


def own_window(block):
    start = max(block * QB - MOST, 0)
    return slice(start, start + WIN)


def fold_rows(part, combine):
    return combine(part.reshape(part.shape[0] // 8, 8, part.shape[1]), axis=0)


def skewed(items, *stages):
    for step in range(len(items) + len(stages) - 1):
        for delay, stage in enumerate(stages):
            if 0 <= step - delay < len(items):
                stage(step - delay, *items[step - delay])


def attention_kernel(
    prefix,
    task_ref,
    seg_ref,
    q_ref,
    k_ref,
    v_ref,
    pk_ref,
    pv_ref,
    *refs,
):
    out_ref, probs_ref, bias, by_key, work = refs
    micro = pl.program_id(0)

    @pl.when(pl.program_id(1) == 0)
    def _():
        fill_mask(seg_ref, task_ref, micro, prefix, bias, by_key)

    height = work.shape[1]
    pieces = [slice(c, c + CHUNK) for c in range(0, height, CHUNK)]

    def scores(index, group, block):
        lanes = slice(group * LANES, (group + 1) * LANES)
        keys = jnp.concatenate([k_ref[own_window(block), lanes], pk_ref[:, lanes]], axis=0)
        queries = stack_heads(q_ref[block * QB : (block + 1) * QB, lanes])
        work[index % 2] = dot_nt(keys, queries)

    def softmax(index, group, block):
        slot = work.at[index % 2]
        top = None
        for piece in pieces:
            hidden = bias[block, piece, :]
            part = slot[piece, :] + jnp.concatenate([hidden, hidden], axis=1)
            slot[piece, :] = part
            part = fold_rows(part, jnp.max)
            top = part if top is None else jnp.maximum(top, part)
        top = jnp.max(top, axis=0, keepdims=True)
        total = None
        for piece in pieces:
            part = jnp.exp2(slot[piece, :] - top)
            slot[piece, :] = part
            part = fold_rows(part, jnp.sum)
            total = part if total is None else total + part
        inverse = 1.0 / jnp.sum(total, axis=0, keepdims=True)
        for piece in pieces:
            probs_ref[group, block, piece, :] = (slot[piece, :] * inverse).astype(bf16)

    def attend(index, group, block):
        lanes = slice(group * LANES, (group + 1) * LANES)
        values = jnp.concatenate([v_ref[own_window(block), lanes], pv_ref[:, lanes]], axis=0)
        result = pick_heads(dot_tn(probs_ref[group, block], values))
        out_ref[block * QB : (block + 1) * QB, lanes] = result.astype(bf16)

    items = [
        (group, block)
        for group in range(q_ref.shape[1] // LANES)
        for block in range(q_ref.shape[0] // QB)
    ]
    skewed(items, scores, softmax, attend)


def attention_call(mixed, segments, tasks, states, prefix):
    micro, _, seq = segments.shape
    width = mixed.shape[1] // 3
    groups = width // LANES
    blocks = seq // QB
    keys = WIN + states.shape[0]
    both = 2
    steps = groups // both
    part = lambda offset: pl.BlockSpec((seq, both * LANES), lambda r, g: (r, offset + g))
    piece = lambda offset: pl.BlockSpec(
        (states.shape[0], both * LANES), lambda r, g: (0, offset + g)
    )
    return pl.pallas_call(
        functools.partial(attention_kernel, prefix),
        grid=(micro, steps),
        in_specs=[
            pl.BlockSpec(memory_space=pltpu.SMEM),
            pl.BlockSpec((None, 1, seq), lambda r, g: (r, 0, 0)),
            part(0),
            part(steps),
            part(2 * steps),
            piece(0),
            piece(steps),
        ],
        out_specs=[
            part(0),
            pl.BlockSpec((None, both, blocks, keys, LANES), lambda r, g: (r, g, 0, 0, 0)),
        ],
        out_shape=[
            jax.ShapeDtypeStruct((micro * seq, width), bf16),
            jax.ShapeDtypeStruct((micro, groups, blocks, keys, LANES), bf16),
        ],
        scratch_shapes=[
            pltpu.VMEM((blocks, keys, 128), f32),
            pltpu.VMEM((seq, 128), f32),
            pltpu.VMEM((2, keys, LANES), f32),
        ],
        compiler_params=pltpu.CompilerParams(vmem_limit_bytes=VMEM_LIMIT),
        name="attention",
    )(tasks, segments, mixed, mixed, mixed, states, states)


def mlp_kernel(
    att_ref,
    tok_ref,
    cot_ref,
    wa_ref,
    ba_ref,
    gain_ref,
    shift_ref,
    wf_ref,
    bf_ref,
    wp_ref,
    bp_ref,
    out_ref,
    gres_ref,
    gatt_ref,
    act_all,
    gpre_all,
):
    gain = row_vector(gain_ref)
    resid = tok_ref[...].astype(f32) + dot_nn(att_ref[...], wa_ref[...]) + row_vector(ba_ref)
    unit, inverse = normalise(resid)
    normed = (unit * gain + row_vector(shift_ref)).astype(bf16)
    grad_out = cot_ref[...]
    for start in range(0, wf_ref.shape[1], FF_CHUNK):
        part = slice(start, start + FF_CHUNK)
        pre = dot_nn(normed, wf_ref[:, part]) + row_vector(bf_ref, part)
        act, gpre = gelu_both(pre, dot_nt(grad_out, wp_ref[part, :]))
        act_all[:, part] = act
        gpre_all[:, part] = gpre
    grad_normed = dot_nt(gpre_all[...], wf_ref[...])
    out = resid + dot_nn(act_all[...], wp_ref[...]) + row_vector(bp_ref)
    out_ref[...] = out.astype(bf16)
    grad_resid = grad_out.astype(f32) + norm_backward(grad_normed, gain, unit, inverse)
    grad_branch = grad_resid.astype(bf16)
    gres_ref[...] = grad_branch
    gatt_ref[...] = dot_nt(grad_branch, wa_ref[...]).astype(bf16)


def mlp_call(attended, tokens, cotangent, w_attn, b_attn, gain, shift, w_fc, b_fc, w_proj, b_proj):
    micro, rows, seq, width = tokens.shape
    tile = 256
    per_row = seq // tile
    flat = pl.BlockSpec((tile, width), lambda i: (i, 0))
    deep = pl.BlockSpec(
        (None, None, tile, width),
        lambda i: (i // (rows * per_row), (i // per_row) % rows, i % per_row, 0),
    )
    once = lambda x: pl.BlockSpec(
        x.shape, lambda i: (0,) * x.ndim, pipeline_mode=pl.Buffered(1)
    )
    weights = (w_attn, b_attn, gain, shift, w_fc, b_fc, w_proj, b_proj)
    count = micro * rows * seq
    return pl.pallas_call(
        mlp_kernel,
        grid=(count // tile,),
        in_specs=[flat, deep, deep] + [once(x) for x in weights],
        out_specs=[deep, flat, flat],
        out_shape=[
            jax.ShapeDtypeStruct(tokens.shape, bf16),
            jax.ShapeDtypeStruct((count, width), bf16),
            jax.ShapeDtypeStruct((count, width), bf16),
        ],
        scratch_shapes=[pltpu.VMEM((tile, w_fc.shape[1]), bf16)] * 2,
        compiler_params=pltpu.CompilerParams(vmem_limit_bytes=VMEM_LIMIT),
        name="feed_forward",
    )(attended, tokens, cotangent, *weights)


def attention_grad_kernel(
    q_ref,
    k_ref,
    v_ref,
    pk_ref,
    pv_ref,
    probs_ref,
    g_ref,
    dq_ref,
    dk_ref,
    dv_ref,
    dpk_ref,
    dpv_ref,
    key_sum,
    value_sum,
    prefix_key_sum,
    prefix_value_sum,
    work,
    score_grad,
):
    blocks = q_ref.shape[0] // QB
    pieces = [slice(c, c + CHUNK) for c in range(0, work.shape[1], CHUNK)]

    def prob_grads(index, block):
        values = jnp.concatenate([v_ref[own_window(block), :], pv_ref[...]], axis=0)
        grads = stack_heads(g_ref[block * QB : (block + 1) * QB, :])
        work[index % 2] = dot_nt(values, grads)

    def softmax_grads(index, block):
        slot = work.at[index % 2]
        delta = None
        for piece in pieces:
            part = slot[piece, :] * probs_ref[block, piece, :].astype(f32)
            slot[piece, :] = part
            part = fold_rows(part, jnp.sum)
            delta = part if delta is None else delta + part
        delta = jnp.sum(delta, axis=0, keepdims=True)
        for piece in pieces:
            part = slot[piece, :] - probs_ref[block, piece, :].astype(f32) * delta
            score_grad[index % 2, piece, :] = part.astype(bf16)

    def mixed_grads(index, block):
        rows = slice(block * QB, (block + 1) * QB)
        window = own_window(block)
        keys = jnp.concatenate([k_ref[window, :], pk_ref[...]], axis=0)
        back = score_grad[index % 2]
        dv = dot_nn(probs_ref[block], stack_heads(g_ref[rows, :]))
        dk = dot_nn(back, stack_heads(q_ref[rows, :]))
        dq = pick_heads(dot_tn(back, keys))
        dq_ref[rows, :] = (dq * HEAD_DIM ** (-0.5)).astype(bf16)
        start = window.start
        old = 0 if block == 0 else block * QB - start if start else WIN
        for total, fresh in ((key_sum, dk), (value_sum, dv)):
            if old:
                total[start : start + old, :] += fresh[:old]
            if old < WIN:
                total[start + old : start + WIN, :] = fresh[old:WIN]
        for total, fresh in ((prefix_key_sum, dk), (prefix_value_sum, dv)):
            if block == 0:
                total[...] = fresh[WIN:]
            else:
                total[...] += fresh[WIN:]
        done = slice(start, window.stop if block == blocks - 1 else start + QB if block >= 2 else 0)
        if done.stop > done.start:
            dk_ref[done, :] = (key_sum[done, :] * LN2).astype(bf16)
            dv_ref[done, :] = value_sum[done, :].astype(bf16)

    skewed([(block,) for block in range(blocks)], prob_grads, softmax_grads, mixed_grads)

    @pl.when(pl.program_id(1) == 0)
    def _():
        dpk_ref[...] = prefix_key_sum[...] * LN2
        dpv_ref[...] = prefix_value_sum[...]

    @pl.when(pl.program_id(1) != 0)
    def _():
        dpk_ref[...] += prefix_key_sum[...] * LN2
        dpv_ref[...] += prefix_value_sum[...]


def attention_grad_call(mixed, states, probs, grad_attended):
    micro, groups, blocks, keys, _ = probs.shape
    seq = blocks * QB
    width = grad_attended.shape[1]
    prefix_rows = states.shape[0]
    part = lambda offset: pl.BlockSpec((seq, LANES), lambda g, r: (r, offset + g))
    piece = lambda offset: pl.BlockSpec((prefix_rows, LANES), lambda g, r: (0, offset + g))
    return pl.pallas_call(
        attention_grad_kernel,
        grid=(groups, micro),
        in_specs=[
            part(0),
            part(groups),
            part(2 * groups),
            piece(0),
            piece(groups),
            pl.BlockSpec((None, None, blocks, keys, LANES), lambda g, r: (r, g, 0, 0, 0)),
            part(0),
        ],
        out_specs=[part(0)] * 3 + [piece(0)] * 2,
        out_shape=[jax.ShapeDtypeStruct((micro * seq, width), bf16)] * 3
        + [jax.ShapeDtypeStruct((prefix_rows, width), f32)] * 2,
        scratch_shapes=[pltpu.VMEM((seq, LANES), f32)] * 2
        + [pltpu.VMEM((prefix_rows, LANES), f32)] * 2
        + [pltpu.VMEM((2, keys, LANES), f32), pltpu.VMEM((2, keys, LANES), bf16)],
        compiler_params=pltpu.CompilerParams(vmem_limit_bytes=VMEM_LIMIT),
        name="attention_grad",
    )(mixed, mixed, mixed, states, states, probs, grad_attended)


def sum_kernel(
    tasks,
    shards,
    dq_ref,
    dk_ref,
    dv_ref,
    tok_ref,
    gres_ref,
    gain_ref,
    w_hbm,
    dpk_ref,
    dpv_ref,
    grad_ref,
    summed_ref,
    w_ref,
    send_a,
    recv_a,
    send_b,
    recv_b,
    gathered,
    load_sem,
    sems,
    sems_b,
):
    step = pl.program_id(0)
    last = pl.num_programs(0) - 1
    shard = lax.axis_index("batch")
    task = lax.axis_index("task")
    task_peers = [(shard, lax.rem(task + k, tasks)) for k in range(1, tasks)]
    shard_peers = [(lax.rem(shard + k, shards), task) for k in range(1, shards)]
    width = dpk_ref.shape[1]
    lanes = send_b.shape[2]
    load = pltpu.make_async_copy(w_hbm, w_ref, load_sem)

    def to_task(k):
        return pltpu.make_async_remote_copy(
            src_ref=send_a.at[lax.rem(task + k, tasks)],
            dst_ref=recv_a.at[k - 1],
            send_sem=sems.at[0, k - 1],
            recv_sem=sems.at[1, k - 1],
            device_id=task_peers[k - 1],
            device_id_type=MESH,
        )

    def to_shard(k):
        return pltpu.make_async_remote_copy(
            src_ref=send_b.at[lax.rem(shard + k, shards)],
            dst_ref=recv_b.at[k - 1],
            send_sem=sems_b.at[0, k - 1],
            recv_sem=sems_b.at[1, k - 1],
            device_id=shard_peers[k - 1],
            device_id_type=MESH,
        )

    def back_to_shard(k):
        return pltpu.make_async_remote_copy(
            src_ref=gathered.at[shard],
            dst_ref=gathered.at[shard],
            send_sem=sems_b.at[2, k - 1],
            recv_sem=sems_b.at[3, k - 1],
            device_id=shard_peers[k - 1],
            device_id_type=MESH,
        )

    def start_tasks():
        pl.semaphore_wait(pltpu.get_barrier_semaphore(), tasks - 1 + shards - 1)
        for k in range(1, tasks):
            to_task(k).start()

    def start_shards():
        for k in range(1, tasks):
            to_task(k).wait()
        total = send_a[task].astype(f32)
        for k in range(1, tasks):
            total = total + recv_a[k - 1].astype(f32)
        total = total.astype(bf16)
        for c in range(shards):
            send_b[c] = total[:, c * lanes : (c + 1) * lanes]
        for k in range(1, shards):
            to_shard(k).start()

    def start_back():
        for k in range(1, shards):
            to_shard(k).wait()
        total = send_b[shard].astype(f32)
        for k in range(1, shards):
            total = total + recv_b[k - 1].astype(f32)
        gathered[shard] = total.astype(bf16)
        for k in range(1, shards):
            back_to_shard(k).start()

    @pl.when(step == 0)
    def _():
        load.start()
        barrier_with(task_peers + shard_peers)
        for t in range(tasks):
            part = slice(t * PAD, (t + 1) * PAD)
            send_a[t, :, :width] = dpk_ref[part, :].astype(bf16)
            send_a[t, :, width:] = dpv_ref[part, :].astype(bf16)
        load.wait()

    @pl.when(step == 1)
    def _():
        start_tasks()

    @pl.when(step == 2)
    def _():
        start_shards()

    @pl.when(step == 3)
    def _():
        start_back()

    grad = dot_nt(dq_ref[...], w_ref[:, :width])
    grad = grad + dot_nt(dk_ref[...], w_ref[:, width : 2 * width])
    grad = grad + dot_nt(dv_ref[...], w_ref[:, 2 * width :])
    unit, inverse = normalise(tok_ref[...].astype(f32))
    back = norm_backward(grad, row_vector(gain_ref), unit, inverse)
    grad_ref[...] = (gres_ref[...].astype(f32) + back).astype(bf16)

    @pl.when(step == last)
    def _():
        for k in range(1, shards):
            back_to_shard(k).wait()
        for c in range(shards):
            summed_ref[:, c * lanes : (c + 1) * lanes] = gathered[c]


def sum_call(tasks, shards, tiles, tile, dq, dk, dv, tokens, grad_resid, gain, w_qkv, dpk, dpv):
    seq, width = tokens.shape[2:]
    per_row = seq // tile
    assert tiles >= 4
    flat = pl.BlockSpec((tile, width), lambda i: (i, 0))
    lanes = 2 * width // shards
    whole = lambda x: pl.BlockSpec(x.shape, lambda i: (0,) * x.ndim)
    return pl.pallas_call(
        functools.partial(sum_kernel, tasks, shards),
        grid=(tiles,),
        in_specs=[flat, flat, flat]
        + [
            pl.BlockSpec((None, None, tile, width), lambda i: (i // per_row, 0, i % per_row, 0)),
            flat,
            whole(gain),
            pl.BlockSpec(memory_space=pl.ANY),
            whole(dpk),
            whole(dpv),
        ],
        out_specs=[flat, pl.BlockSpec((PAD, 2 * width), lambda i: (0, 0))],
        out_shape=[
            jax.ShapeDtypeStruct((tiles * tile, width), bf16),
            jax.ShapeDtypeStruct((PAD, 2 * width), bf16),
        ],
        scratch_shapes=[
            pltpu.VMEM(w_qkv.shape, bf16),
            pltpu.VMEM((tasks, PAD, 2 * width), bf16),
            pltpu.VMEM((tasks - 1, PAD, 2 * width), bf16),
            pltpu.VMEM((shards, PAD, lanes), bf16),
            pltpu.VMEM((shards - 1, PAD, lanes), bf16),
            pltpu.VMEM((shards, PAD, lanes), bf16),
            pltpu.SemaphoreType.DMA,
            pltpu.SemaphoreType.DMA((2, tasks - 1)),
            pltpu.SemaphoreType.DMA((4, shards - 1)),
        ],
        compiler_params=pltpu.CompilerParams(
            collective_id=1, has_side_effects=True, vmem_limit_bytes=VMEM_LIMIT
        ),
        name="grad_first_sum",
    )(dq, dk, dv, tokens, grad_resid, gain, w_qkv, dpk, dpv)


def last_kernel(
    grad_hbm,
    summed_ref,
    hidden_ref,
    embed_ref,
    win_hbm,
    wout_hbm,
    out_hbm,
    gembed_ref,
    gin_hbm,
    gbin_ref,
    gout_hbm,
    gbout_ref,
    win_ref,
    wout_ref,
    held,
    padded,
    gin,
    gout,
    sems,
):
    seq = out_hbm.shape[2]
    load_in = pltpu.make_async_copy(win_hbm.at[0], win_ref, sems.at[0])
    load_out = pltpu.make_async_copy(wout_hbm.at[0], wout_ref, sems.at[1])
    put_in = pltpu.make_async_copy(gin, gin_hbm.at[0], sems.at[2])
    put_out = pltpu.make_async_copy(gout, gout_hbm.at[0], sems.at[3])
    takes, puts = [], []
    for index in range(out_hbm.shape[0]):
        rows = pl.ds(index * seq, seq)
        takes.append(
            pltpu.make_async_copy(grad_hbm.at[rows, :], held.at[rows, :], sems.at[4 + 2 * index])
        )
        puts.append(
            pltpu.make_async_copy(held.at[rows, :], out_hbm.at[index, 0], sems.at[5 + 2 * index])
        )
    for load in [load_out, load_in] + takes:
        load.start()
    summed = summed_ref[...]
    hidden = hidden_ref[...]
    gout[...] = dot_tn(hidden.astype(bf16), summed)
    put_out.start()
    gbout_ref[...] = jnp.sum(summed.astype(f32), axis=0, keepdims=True)
    padded[...] = jnp.zeros(padded.shape, f32)
    padded[: embed_ref.shape[1], :] = embed_ref[0].astype(f32)
    load_out.wait()
    load_in.wait()
    grad_hidden = dot_nt(summed, wout_ref[...])
    for take, put in zip(takes, puts):
        take.wait()
        put.start()
    grad_pre = (grad_hidden * (1.0 - hidden * hidden)).astype(bf16)
    gin[...] = dot_tn(padded[...].astype(bf16), grad_pre)
    put_in.start()
    gbin_ref[...] = jnp.sum(grad_pre.astype(f32), axis=0, keepdims=True)
    gembed_ref[:, 0, :] = dot_nt(grad_pre, win_ref[...])[: embed_ref.shape[1], :]
    for copy in puts + [put_in, put_out]:
        copy.wait()


def last_call(grad, shape, summed, hidden, embed, w_in, w_out):
    width = shape[3]
    anywhere = pl.BlockSpec(memory_space=pl.ANY)
    whole = lambda shape: pl.BlockSpec(shape, lambda i: (0,) * len(shape))
    rank = w_in.shape[2]
    prefix = embed.shape[1]
    return pl.pallas_call(
        last_kernel,
        grid=(1,),
        in_specs=[anywhere]
        + [whole(x.shape) for x in (summed, hidden, embed)]
        + [anywhere, anywhere],
        out_specs=[
            anywhere,
            whole((prefix, 1, width)),
            anywhere,
            whole((1, rank)),
            anywhere,
            whole((1, 2 * width)),
        ],
        out_shape=[
            jax.ShapeDtypeStruct(shape, bf16),
            jax.ShapeDtypeStruct((prefix, 1, width), f32),
            jax.ShapeDtypeStruct(w_in.shape, f32),
            jax.ShapeDtypeStruct((1, rank), f32),
            jax.ShapeDtypeStruct(w_out.shape, f32),
            jax.ShapeDtypeStruct((1, 2 * width), f32),
        ],
        scratch_shapes=[
            pltpu.VMEM(w_in.shape[1:], bf16),
            pltpu.VMEM(w_out.shape[1:], bf16),
            pltpu.VMEM(grad.shape, bf16),
            pltpu.VMEM((PAD, width), f32),
            pltpu.VMEM(w_in.shape[1:], f32),
            pltpu.VMEM(w_out.shape[1:], f32),
            pltpu.SemaphoreType.DMA((4 + 2 * shape[0],)),
        ],
        compiler_params=pltpu.CompilerParams(vmem_limit_bytes=VMEM_LIMIT),
        name="grad_last",
    )(grad, summed, hidden, embed, w_in, w_out)


def on_device(
    tasks,
    shards,
    tokens,
    cotangent,
    segment_ids,
    task_ids,
    ln1_gain,
    ln1_bias,
    w_qkv,
    b_qkv,
    w_attn_out,
    b_attn_out,
    ln2_gain,
    ln2_bias,
    w_fc,
    b_fc,
    w_proj,
    b_proj,
    prefix_embed,
    reparam_in,
    reparam_in_bias,
    reparam_out,
    reparam_out_bias,
):
    mixed, hidden, states, *kept = qkv_call(
        tasks,
        tokens,
        ln1_gain,
        ln1_bias,
        w_qkv,
        b_qkv,
        prefix_embed,
        reparam_in,
        reparam_in_bias,
        reparam_out,
        reparam_out_bias,
        (),
    )
    attended, probs = attention_call(
        mixed, segment_ids, task_ids, states, prefix_embed.shape[1]
    )
    block_out, grad_resid, grad_attended = mlp_call(
        attended,
        tokens,
        cotangent,
        w_attn_out,
        b_attn_out,
        ln2_gain,
        ln2_bias,
        w_fc,
        b_fc,
        w_proj,
        b_proj,
    )
    dq, dk, dv, dpk, dpv = attention_grad_call(mixed, states, probs, grad_attended)
    tile = 512
    first, summed = sum_call(
        tasks,
        shards,
        dq.shape[0] // tile,
        tile,
        dq,
        dk,
        dv,
        tokens,
        grad_resid,
        ln1_gain,
        w_qkv,
        dpk,
        dpv,
    )
    input_grad, gembed, gin, gbin, gout, gbout = last_call(
        first, tokens.shape, summed, hidden, prefix_embed, reparam_in, reparam_out
    )
    return (block_out, input_grad, jnp.swapaxes(gembed, 0, 1), gin, gbin, gout, gbout)


def solution(mesh):
    split = ("batch", "task")
    in_specs = (
        (P(None, split, None, None),) * 2
        + (P(None, split, None),) * 2
        + (P(),) * 12
        + (
            P("task", None, None),
            P("task", None, None),
            P("task", None),
            P("task", None, None),
            P("task", None),
        )
    )
    out_specs = (
        P(None, split, None, None),
        P(None, split, None, None),
        P("task", None, None),
        P("task", None, None),
        P("task", None),
        P("task", None, None),
        P("task", None),
    )
    return jax.shard_map(
        functools.partial(on_device, mesh.shape["task"], mesh.shape["batch"]),
        mesh=mesh,
        in_specs=in_specs,
        out_specs=out_specs,
        check_vma=False,
    )
```

```python
import functools

import jax
import jax.numpy as jnp
from jax import lax
from jax.experimental import pallas as pl
from jax.experimental.pallas import tpu as pltpu
from jax.sharding import PartitionSpec as P

bf16 = jnp.bfloat16
f32 = jnp.float32

HEADS = 16
HEAD_DIM = 64
GROUP = 4
LANES = GROUP * HEAD_DIM
QB = 64
MOST = 128
WIN = MOST + QB
PAD = 16
EPSILON = 1e-05
NEGATIVE = -1e30
LOG2E = 1.4426950408889634
LN2 = 0.6931471805599453
GELU_A = 0.7978845608028654
GELU_B = 0.044715
VMEM_LIMIT = 62 << 20
CHUNK = 32
QKV_TILE = 256
FF_CHUNK = 1024
MESH = pl.DeviceIdType.MESH


def dot_nn(left, right):
    return jnp.dot(left, right, preferred_element_type=f32)


def dot_nt(left, right):
    return lax.dot_general(
        left, right, (((1,), (1,)), ((), ())), preferred_element_type=f32
    )


def dot_tn(left, right):
    return lax.dot_general(
        left, right, (((0,), (0,)), ((), ())), preferred_element_type=f32
    )


def row_vector(ref, part=slice(None)):
    return ref[part].astype(f32)[None, :]


def normalise(hidden):
    centred = hidden - jnp.mean(hidden, axis=1, keepdims=True)
    spread = jnp.mean(centred * centred, axis=1, keepdims=True)
    inverse = lax.rsqrt(spread + EPSILON)
    return centred * inverse, inverse


def norm_backward(grad, gain, unit, inverse):
    scaled = grad * gain
    mean_one = jnp.mean(scaled, axis=1, keepdims=True)
    mean_two = jnp.mean(scaled * unit, axis=1, keepdims=True)
    return inverse * (scaled - mean_one - unit * mean_two)


def gelu_both(value, grad):
    square = value * value
    half = 0.5 + 0.5 * jnp.tanh(value * (GELU_A + (GELU_A * GELU_B) * square))
    act = value * half
    slope = half + (act * (2 * GELU_A + (6 * GELU_A * GELU_B) * square)) * (1.0 - half)
    return act.astype(bf16), (grad * slope).astype(bf16)


def barrier_with(peers):
    barrier = pltpu.get_barrier_semaphore()
    for peer in peers:
        pl.semaphore_signal(barrier, inc=1, device_id=peer, device_id_type=MESH)
    return barrier


def qkv_kernel(
    tasks,
    tok_ref,
    gain_ref,
    shift_ref,
    w_hbm,
    b_ref,
    embed_ref,
    win_hbm,
    bin_ref,
    wout_hbm,
    bout_ref,
    mixed_ref,
    hidden_ref,
    states_ref,
    win,
    wout,
    padded,
    own,
    gathered,
    w_ref,
    current,
    load_sem,
    send_sem,
    recv_sem,
):
    step = pl.program_id(0)
    last = pl.num_programs(0) - 1
    row_axis = lax.axis_index("batch")
    me = lax.axis_index("task")
    peers = [(row_axis, lax.rem(me + k, tasks)) for k in range(1, tasks)]

    width = tok_ref.shape[1]

    columns = [slice(part * width, (part + 1) * width) for part in range(3)]
    copies = [(w_hbm.at[:, part], w_ref.at[:, part]) for part in columns]
    copies += [(win_hbm.at[0], win), (wout_hbm.at[0], wout)]

    def load(index):
        return pltpu.make_async_copy(*copies[index], load_sem.at[index])

    def send(k):
        return pltpu.make_async_remote_copy(
            src_ref=own,
            dst_ref=gathered.at[me],
            send_sem=send_sem.at[k - 1],
            recv_sem=recv_sem.at[k - 1],
            device_id=peers[k - 1],
            device_id_type=MESH,
        )

    def norm():
        normed, _ = normalise(tok_ref[...].astype(f32))
        return (normed * row_vector(gain_ref) + row_vector(shift_ref)).astype(bf16)

    @pl.when(step == 0)
    def _():
        for index in range(len(copies)):
            load(index).start()
        barrier_with(peers)
        current[...] = norm()

    @pl.when(step == 2)
    def _():
        load(3).wait()
        load(4).wait()
        padded[...] = jnp.zeros(padded.shape, f32)
        padded[: embed_ref.shape[1], :] = embed_ref[0].astype(f32)
        pre = dot_nn(padded[...].astype(bf16), win[...]) + bin_ref[...].astype(f32)
        hidden = jnp.tanh(pre)
        hidden_ref[...] = hidden
        states = dot_nn(hidden.astype(bf16), wout[...]) + bout_ref[...].astype(f32)
        states = states.astype(bf16)
        own[...] = states
        gathered[me] = states
        pl.semaphore_wait(pltpu.get_barrier_semaphore(), tasks - 1)
        for k in range(1, tasks):
            send(k).start()

    def work(ready):
        following = norm()
        for index, part in enumerate(columns):
            ready(index)
            mixed = dot_nn(current[...], w_ref[:, part]) + row_vector(b_ref, part)
            if index == 0:
                mixed = mixed * (HEAD_DIM ** (-0.5) * LOG2E)
            mixed_ref[:, part] = mixed.astype(bf16)
        current[...] = following

    @pl.when(step == 1)
    def _():
        work(lambda index: load(index).wait())

    @pl.when(step > 1)
    def _():
        work(lambda index: None)

    @pl.when(step == last)
    def _():
        for k in range(1, tasks):
            send(k).wait()
        states_ref[...] = gathered[...].reshape(states_ref.shape)


def qkv_call(tasks, tokens, gain, shift, w_qkv, b_qkv, embed, w_in, b_in, w_out, b_out):
    micro, rows, seq, width = tokens.shape
    tile = QKV_TILE
    per_row = seq // tile
    rank = w_in.shape[2]
    whole1 = lambda x: pl.BlockSpec(x.shape, lambda i: (0,) * x.ndim)
    tiles = micro * rows * per_row
    ahead = lambda i: jnp.minimum(i, tiles - 1)
    return pl.pallas_call(
        functools.partial(qkv_kernel, tasks),
        grid=(tiles + 1,),
        in_specs=[
            pl.BlockSpec(
                (None, None, tile, width),
                lambda i: (
                    ahead(i) // (rows * per_row),
                    lax.rem(ahead(i) // per_row, rows),
                    lax.rem(ahead(i), per_row),
                    0,
                ),
            ),
            whole1(gain),
            whole1(shift),
            pl.BlockSpec(memory_space=pl.ANY),
            whole1(b_qkv),
            whole1(embed),
            pl.BlockSpec(memory_space=pl.ANY),
            whole1(b_in),
            pl.BlockSpec(memory_space=pl.ANY),
            whole1(b_out),
        ],
        out_specs=[
            pl.BlockSpec((tile, 3 * width), lambda i: (jnp.maximum(i - 1, 0), 0)),
            pl.BlockSpec((PAD, rank), lambda i: (0, 0)),
            pl.BlockSpec((tasks * PAD, 2 * width), lambda i: (0, 0)),
        ],
        out_shape=[
            jax.ShapeDtypeStruct((micro * rows * seq, 3 * width), bf16),
            jax.ShapeDtypeStruct((PAD, rank), f32),
            jax.ShapeDtypeStruct((tasks * PAD, 2 * width), bf16),
        ],
        scratch_shapes=[
            pltpu.VMEM(w_in.shape[1:], bf16),
            pltpu.VMEM(w_out.shape[1:], bf16),
            pltpu.VMEM((PAD, width), f32),
            pltpu.VMEM((PAD, 2 * width), bf16),
            pltpu.VMEM((tasks, PAD, 2 * width), bf16),
            pltpu.VMEM(w_qkv.shape, bf16),
            pltpu.VMEM((tile, width), bf16),
            pltpu.SemaphoreType.DMA((5,)),
            pltpu.SemaphoreType.DMA((tasks - 1,)),
            pltpu.SemaphoreType.DMA((tasks - 1,)),
        ],
        compiler_params=pltpu.CompilerParams(
            collective_id=0, has_side_effects=True, vmem_limit_bytes=VMEM_LIMIT
        ),
        name="norm_qkv",
    )(tokens, gain, shift, w_qkv, b_qkv, embed, w_in, b_in, w_out, b_out)


def stack_heads(block):
    lane = lax.broadcasted_iota(jnp.int32, (QB, 128), 1)
    zero = jnp.zeros((QB, 128), block.dtype)
    rows = []
    for h in range(GROUP):
        part = jnp.where((lane < HEAD_DIM) == (h % 2 == 0), block[:, (h // 2) * 128 :][:, :128], zero)
        rows.append(jnp.concatenate([part, zero] if h < 2 else [zero, part], axis=1))
    return jnp.concatenate(rows, axis=0)


def pick_heads(stacked):
    lane = lax.broadcasted_iota(jnp.int32, (QB, 128), 1)
    low = jnp.where(lane < HEAD_DIM, stacked[:QB, :128], stacked[QB : 2 * QB, :128])
    high = jnp.where(lane < HEAD_DIM, stacked[2 * QB : 3 * QB, 128:], stacked[3 * QB :, 128:])
    return jnp.concatenate([low, high], axis=1)


def fill_mask(seg_ref, task_ref, micro, prefix, bias, by_key):
    segments = seg_ref[...]
    seq = segments.shape[1]
    token_task = jnp.zeros(segments.shape, jnp.int32)
    for s in range(task_ref.shape[-1]):
        token_task = jnp.where(segments == s, task_ref[micro, 0, s], token_task)
    segments = segments.astype(f32)
    for c in range(0, seq, 128):
        by_key[c : c + 128, :] = jnp.broadcast_to(segments[:, c : c + 128], (128, 128)).T
    for b in range(seq // QB):
        start = max(b * QB - MOST, 0)

        def twice(x):
            part = x[:, b * QB : (b + 1) * QB]
            return jnp.concatenate([part, part], axis=1)

        key_pos = start + lax.broadcasted_iota(jnp.int32, (WIN, 128), 0)
        query_pos = b * QB + (lax.broadcasted_iota(jnp.int32, (WIN, 128), 1) & (QB - 1))
        own = (by_key[start : start + WIN, :] == twice(segments)) & (key_pos <= query_pos)
        bias[b, :WIN, :] = jnp.where(own, 0.0, NEGATIVE)
        index = lax.broadcasted_iota(jnp.int32, (bias.shape[1] - WIN, 128), 0)
        fits = (lax.shift_right_logical(index, 4) == twice(token_task)) & (
            (index & (PAD - 1)) < prefix
        )
        bias[b, WIN:, :] = jnp.where(fits, 0.0, NEGATIVE)


def own_window(block):
    start = max(block * QB - MOST, 0)
    return slice(start, start + WIN)


def fold_rows(part, combine):
    return combine(part.reshape(part.shape[0] // 8, 8, part.shape[1]), axis=0)


def skewed(items, *stages):
    for step in range(len(items) + len(stages) - 1):
        for delay, stage in enumerate(stages):
            if 0 <= step - delay < len(items):
                stage(step - delay, *items[step - delay])


def attention_feed_kernel(
    prefix,
    units,
    task_ref,
    seg_ref,
    q_ref,
    k_ref,
    v_ref,
    pk_ref,
    pv_ref,
    tok_ref,
    cot_ref,
    wa_hbm,
    ba_ref,
    gain_ref,
    shift_ref,
    wf_hbm,
    bf_ref,
    wp_hbm,
    bp_ref,
    probs_ref,
    out_ref,
    gres_ref,
    gatt_ref,
    bias,
    by_key,
    work,
    attended,
    act_all,
    gpre_all,
    wa_ref,
    wf_ref,
    wp_ref,
    weight_sem,
):
    step = pl.program_id(0)
    groups = attended.shape[1]
    unit = jnp.minimum(step, units - 1)
    micro = unit // groups
    group = lax.rem(unit, groups)
    loads = [
        pltpu.make_async_copy(source, target, weight_sem.at[index])
        for index, (source, target) in enumerate(
            ((wa_hbm, wa_ref), (wf_hbm, wf_ref), (wp_hbm, wp_ref))
        )
    ]

    for index in range(len(loads)):

        @pl.when(step == 1 + 2 * index)
        def _():
            loads[index].start()

    @pl.when((step < units) & (group == 0))
    def _():
        fill_mask(seg_ref, task_ref, micro, prefix, bias, by_key)

    pieces = [slice(c, c + CHUNK) for c in range(0, work.shape[1], CHUNK)]

    def scores(index, block):
        keys = jnp.concatenate([k_ref[own_window(block), :], pk_ref[...]], axis=0)
        queries = stack_heads(q_ref[block * QB : (block + 1) * QB, :])
        work[index % 2] = dot_nt(keys, queries)

    def softmax(index, block):
        slot = work.at[index % 2]
        top = None
        for piece in pieces:
            hidden = bias[block, piece, :]
            part = slot[piece, :] + jnp.concatenate([hidden, hidden], axis=1)
            slot[piece, :] = part
            part = fold_rows(part, jnp.max)
            top = part if top is None else jnp.maximum(top, part)
        top = jnp.max(top, axis=0, keepdims=True)
        total = None
        for piece in pieces:
            part = jnp.exp2(slot[piece, :] - top)
            slot[piece, :] = part
            part = fold_rows(part, jnp.sum)
            total = part if total is None else total + part
        inverse = 1.0 / jnp.sum(total, axis=0, keepdims=True)
        for piece in pieces:
            probs_ref[block, piece, :] = (slot[piece, :] * inverse).astype(bf16)

    def attend(index, block):
        values = jnp.concatenate([v_ref[own_window(block), :], pv_ref[...]], axis=0)
        result = pick_heads(dot_tn(probs_ref[block], values))
        attended[micro, group, block * QB : (block + 1) * QB, :] = result.astype(bf16)

    @pl.when(step < units)
    def _():
        blocks = [(block,) for block in range(q_ref.shape[0] // QB)]
        skewed(blocks, scores, softmax, attend)

    @pl.when(step == units)
    def _():
        for load in loads:
            load.wait()

    @pl.when(step >= units)
    def _():
        tile = tok_ref.shape[0]
        per_row = attended.shape[2] // tile
        index = jnp.maximum(step - units, 0)
        rows = pl.ds(pl.multiple_of(lax.rem(index, per_row) * tile, tile), tile)
        tile_attended = jnp.concatenate(
            [attended[index // per_row, g, rows, :] for g in range(groups)], axis=1
        )
        gain = row_vector(gain_ref)
        resid = tok_ref[...].astype(f32) + dot_nn(tile_attended, wa_ref[...]) + row_vector(ba_ref)
        unit_norm, inverse = normalise(resid)
        normed = (unit_norm * gain + row_vector(shift_ref)).astype(bf16)
        grad_out = cot_ref[...]
        for start in range(0, wf_ref.shape[1], FF_CHUNK):
            part = slice(start, start + FF_CHUNK)
            pre = dot_nn(normed, wf_ref[:, part]) + row_vector(bf_ref, part)
            act, gpre = gelu_both(pre, dot_nt(grad_out, wp_ref[part, :]))
            act_all[:, part] = act
            gpre_all[:, part] = gpre
        grad_normed = dot_nt(gpre_all[...], wf_ref[...])
        out = resid + dot_nn(act_all[...], wp_ref[...]) + row_vector(bp_ref)
        out_ref[...] = out.astype(bf16)
        grad_resid = grad_out.astype(f32) + norm_backward(grad_normed, gain, unit_norm, inverse)
        grad_branch = grad_resid.astype(bf16)
        gres_ref[...] = grad_branch
        gatt_ref[...] = dot_nt(grad_branch, wa_ref[...]).astype(bf16)


def attention_feed_call(
    mixed, segments, tasks, states, prefix, tokens, cotangent, weights
):
    micro, _, seq, width = tokens.shape
    groups = width // LANES
    blocks = seq // QB
    prefix_rows = states.shape[0]
    keys = WIN + prefix_rows
    units = micro * groups
    tile = 256
    per_row = seq // tile
    count = micro * seq
    w_attn, _, _, _, w_fc, _, w_proj, _ = weights
    unit = lambda i: jnp.minimum(i, units - 1)
    index = lambda i: jnp.maximum(i - units, 0)
    part = lambda offset: pl.BlockSpec(
        (seq, LANES), lambda i: (unit(i) // groups, offset + lax.rem(unit(i), groups))
    )
    piece = lambda offset: pl.BlockSpec(
        (prefix_rows, LANES), lambda i: (0, offset + lax.rem(unit(i), groups))
    )
    flat = pl.BlockSpec((tile, width), lambda i: (index(i), 0))
    deep = pl.BlockSpec(
        (None, None, tile, width),
        lambda i: (index(i) // per_row, 0, lax.rem(index(i), per_row), 0),
    )

    def weight(x):
        if x.ndim == 2:
            return pl.BlockSpec(memory_space=pl.ANY)
        return pl.BlockSpec(x.shape, lambda i: (0,))

    return pl.pallas_call(
        functools.partial(attention_feed_kernel, prefix, units),
        grid=(units + count // tile,),
        in_specs=[
            pl.BlockSpec(memory_space=pltpu.SMEM),
            pl.BlockSpec((None, 1, seq), lambda i: (unit(i) // groups, 0, 0)),
            part(0),
            part(groups),
            part(2 * groups),
            piece(0),
            piece(groups),
            deep,
            deep,
        ]
        + [weight(x) for x in weights],
        out_specs=[
            pl.BlockSpec(
                (None, None, blocks, keys, LANES),
                lambda i: (unit(i) // groups, lax.rem(unit(i), groups), 0, 0, 0),
            ),
            deep,
            flat,
            flat,
        ],
        out_shape=[
            jax.ShapeDtypeStruct((micro, groups, blocks, keys, LANES), bf16),
            jax.ShapeDtypeStruct(tokens.shape, bf16),
            jax.ShapeDtypeStruct((count, width), bf16),
            jax.ShapeDtypeStruct((count, width), bf16),
        ],
        scratch_shapes=[
            pltpu.VMEM((blocks, keys, 128), f32),
            pltpu.VMEM((seq, 128), f32),
            pltpu.VMEM((2, keys, LANES), f32),
            pltpu.VMEM((micro, groups, seq, LANES), bf16),
            pltpu.VMEM((tile, w_fc.shape[1]), bf16),
            pltpu.VMEM((tile, w_fc.shape[1]), bf16),
        ]
        + [pltpu.VMEM(x.shape, bf16) for x in (w_attn, w_fc, w_proj)]
        + [pltpu.SemaphoreType.DMA((3,))],
        compiler_params=pltpu.CompilerParams(vmem_limit_bytes=VMEM_LIMIT),
        name="attention_feed",
    )(tasks, segments, mixed, mixed, mixed, states, states, tokens, cotangent, *weights)


def attention_grad_kernel(
    q_ref,
    k_ref,
    v_ref,
    pk_ref,
    pv_ref,
    probs_ref,
    g_ref,
    dq_ref,
    dk_ref,
    dv_ref,
    dpk_ref,
    dpv_ref,
    key_sum,
    value_sum,
    prefix_key_sum,
    prefix_value_sum,
    work,
    score_grad,
):
    blocks = q_ref.shape[0] // QB
    pieces = [slice(c, c + CHUNK) for c in range(0, work.shape[1], CHUNK)]

    def prob_grads(index, block):
        values = jnp.concatenate([v_ref[own_window(block), :], pv_ref[...]], axis=0)
        grads = stack_heads(g_ref[block * QB : (block + 1) * QB, :])
        work[index % 2] = dot_nt(values, grads)

    def softmax_grads(index, block):
        slot = work.at[index % 2]
        delta = None
        for piece in pieces:
            part = slot[piece, :] * probs_ref[block, piece, :].astype(f32)
            slot[piece, :] = part
            part = fold_rows(part, jnp.sum)
            delta = part if delta is None else delta + part
        delta = jnp.sum(delta, axis=0, keepdims=True)
        for piece in pieces:
            part = slot[piece, :] - probs_ref[block, piece, :].astype(f32) * delta
            score_grad[index % 2, piece, :] = part.astype(bf16)

    def mixed_grads(index, block):
        rows = slice(block * QB, (block + 1) * QB)
        window = own_window(block)
        keys = jnp.concatenate([k_ref[window, :], pk_ref[...]], axis=0)
        back = score_grad[index % 2]
        dv = dot_nn(probs_ref[block], stack_heads(g_ref[rows, :]))
        dk = dot_nn(back, stack_heads(q_ref[rows, :]))
        dq = pick_heads(dot_tn(back, keys))
        dq_ref[rows, :] = (dq * HEAD_DIM ** (-0.5)).astype(bf16)
        start = window.start
        old = 0 if block == 0 else block * QB - start if start else WIN
        for total, fresh in ((key_sum, dk), (value_sum, dv)):
            if old:
                total[start : start + old, :] += fresh[:old]
            if old < WIN:
                total[start + old : start + WIN, :] = fresh[old:WIN]
        for total, fresh in ((prefix_key_sum, dk), (prefix_value_sum, dv)):
            if block == 0:
                total[...] = fresh[WIN:]
            else:
                total[...] += fresh[WIN:]
        done = slice(start, window.stop if block == blocks - 1 else start + QB if block >= 2 else 0)
        if done.stop > done.start:
            dk_ref[done, :] = (key_sum[done, :] * LN2).astype(bf16)
            dv_ref[done, :] = value_sum[done, :].astype(bf16)

    skewed([(block,) for block in range(blocks)], prob_grads, softmax_grads, mixed_grads)

    @pl.when(pl.program_id(1) == 0)
    def _():
        dpk_ref[...] = prefix_key_sum[...] * LN2
        dpv_ref[...] = prefix_value_sum[...]

    @pl.when(pl.program_id(1) != 0)
    def _():
        dpk_ref[...] += prefix_key_sum[...] * LN2
        dpv_ref[...] += prefix_value_sum[...]


def attention_grad_call(mixed, states, probs, grad_attended):
    micro, groups, blocks, keys, _ = probs.shape
    seq = blocks * QB
    width = grad_attended.shape[1]
    prefix_rows = states.shape[0]
    part = lambda offset: pl.BlockSpec((seq, LANES), lambda g, r: (r, offset + g))
    piece = lambda offset: pl.BlockSpec((prefix_rows, LANES), lambda g, r: (0, offset + g))
    return pl.pallas_call(
        attention_grad_kernel,
        grid=(groups, micro),
        in_specs=[
            part(0),
            part(groups),
            part(2 * groups),
            piece(0),
            piece(groups),
            pl.BlockSpec((None, None, blocks, keys, LANES), lambda g, r: (r, g, 0, 0, 0)),
            part(0),
        ],
        out_specs=[part(0)] * 3 + [piece(0)] * 2,
        out_shape=[jax.ShapeDtypeStruct((micro * seq, width), bf16)] * 3
        + [jax.ShapeDtypeStruct((prefix_rows, width), f32)] * 2,
        scratch_shapes=[pltpu.VMEM((seq, LANES), f32)] * 2
        + [pltpu.VMEM((prefix_rows, LANES), f32)] * 2
        + [pltpu.VMEM((2, keys, LANES), f32), pltpu.VMEM((2, keys, LANES), bf16)],
        compiler_params=pltpu.CompilerParams(vmem_limit_bytes=VMEM_LIMIT),
        name="attention_grad",
    )(mixed, mixed, mixed, states, states, probs, grad_attended)


def sum_kernel(
    tasks,
    shards,
    dq_ref,
    dk_ref,
    dv_ref,
    tok_ref,
    gres_ref,
    gain_ref,
    w_hbm,
    dpk_ref,
    dpv_ref,
    grad_ref,
    summed_ref,
    w_ref,
    send_a,
    recv_a,
    send_b,
    recv_b,
    gathered,
    load_sem,
    sems,
    sems_b,
):
    step = pl.program_id(0)
    last = pl.num_programs(0) - 1
    shard = lax.axis_index("batch")
    task = lax.axis_index("task")
    task_peers = [(shard, lax.rem(task + k, tasks)) for k in range(1, tasks)]
    shard_peers = [(lax.rem(shard + k, shards), task) for k in range(1, shards)]
    width = dpk_ref.shape[1]
    lanes = send_b.shape[2]
    loads = [
        pltpu.make_async_copy(
            w_hbm.at[:, index * width : (index + 1) * width],
            w_ref.at[:, index * width : (index + 1) * width],
            load_sem.at[index],
        )
        for index in range(3)
    ]

    def to_task(k):
        return pltpu.make_async_remote_copy(
            src_ref=send_a.at[lax.rem(task + k, tasks)],
            dst_ref=recv_a.at[k - 1],
            send_sem=sems.at[0, k - 1],
            recv_sem=sems.at[1, k - 1],
            device_id=task_peers[k - 1],
            device_id_type=MESH,
        )

    def to_shard(k):
        return pltpu.make_async_remote_copy(
            src_ref=send_b.at[lax.rem(shard + k, shards)],
            dst_ref=recv_b.at[k - 1],
            send_sem=sems_b.at[0, k - 1],
            recv_sem=sems_b.at[1, k - 1],
            device_id=shard_peers[k - 1],
            device_id_type=MESH,
        )

    def back_to_shard(k):
        return pltpu.make_async_remote_copy(
            src_ref=gathered.at[shard],
            dst_ref=gathered.at[shard],
            send_sem=sems_b.at[2, k - 1],
            recv_sem=sems_b.at[3, k - 1],
            device_id=shard_peers[k - 1],
            device_id_type=MESH,
        )

    def start_tasks():
        pl.semaphore_wait(pltpu.get_barrier_semaphore(), tasks - 1 + shards - 1)
        for k in range(1, tasks):
            to_task(k).start()

    def start_shards():
        for k in range(1, tasks):
            to_task(k).wait()
        total = send_a[task].astype(f32)
        for k in range(1, tasks):
            total = total + recv_a[k - 1].astype(f32)
        total = total.astype(bf16)
        for c in range(shards):
            send_b[c] = total[:, c * lanes : (c + 1) * lanes]
        for k in range(1, shards):
            to_shard(k).start()

    def start_back():
        for k in range(1, shards):
            to_shard(k).wait()
        total = send_b[shard].astype(f32)
        for k in range(1, shards):
            total = total + recv_b[k - 1].astype(f32)
        gathered[shard] = total.astype(bf16)
        for k in range(1, shards):
            back_to_shard(k).start()

    @pl.when(step == 0)
    def _():
        for load in loads:
            load.start()
        barrier_with(task_peers + shard_peers)
        for t in range(tasks):
            part = slice(t * PAD, (t + 1) * PAD)
            send_a[t, :, :width] = dpk_ref[part, :].astype(bf16)
            send_a[t, :, width:] = dpv_ref[part, :].astype(bf16)

    @pl.when(step == 1)
    def _():
        start_tasks()

    @pl.when(step == 2)
    def _():
        start_shards()

    @pl.when(step == 3)
    def _():
        start_back()

    def work(ready):
        grad = 0.0
        for index, part in enumerate((dq_ref, dk_ref, dv_ref)):
            ready(index)
            grad = grad + dot_nt(part[...], w_ref[:, index * width : (index + 1) * width])
        unit, inverse = normalise(tok_ref[...].astype(f32))
        back = norm_backward(grad, row_vector(gain_ref), unit, inverse)
        grad_ref[...] = (gres_ref[...].astype(f32) + back).astype(bf16)

    @pl.when(step == 0)
    def _():
        work(lambda index: loads[index].wait())

    @pl.when(step > 0)
    def _():
        work(lambda index: None)

    @pl.when(step == last)
    def _():
        for k in range(1, shards):
            back_to_shard(k).wait()
        for c in range(shards):
            summed_ref[:, c * lanes : (c + 1) * lanes] = gathered[c]


def sum_call(tasks, shards, tiles, tile, dq, dk, dv, tokens, grad_resid, gain, w_qkv, dpk, dpv):
    seq, width = tokens.shape[2:]
    per_row = seq // tile
    assert tiles >= 4
    flat = pl.BlockSpec((tile, width), lambda i: (i, 0))
    lanes = 2 * width // shards
    whole = lambda x: pl.BlockSpec(x.shape, lambda i: (0,) * x.ndim)
    return pl.pallas_call(
        functools.partial(sum_kernel, tasks, shards),
        grid=(tiles,),
        in_specs=[flat, flat, flat]
        + [
            pl.BlockSpec((None, None, tile, width), lambda i: (i // per_row, 0, i % per_row, 0)),
            flat,
            whole(gain),
            pl.BlockSpec(memory_space=pl.ANY),
            whole(dpk),
            whole(dpv),
        ],
        out_specs=[flat, pl.BlockSpec((PAD, 2 * width), lambda i: (0, 0))],
        out_shape=[
            jax.ShapeDtypeStruct((tiles * tile, width), bf16),
            jax.ShapeDtypeStruct((PAD, 2 * width), bf16),
        ],
        scratch_shapes=[
            pltpu.VMEM(w_qkv.shape, bf16),
            pltpu.VMEM((tasks, PAD, 2 * width), bf16),
            pltpu.VMEM((tasks - 1, PAD, 2 * width), bf16),
            pltpu.VMEM((shards, PAD, lanes), bf16),
            pltpu.VMEM((shards - 1, PAD, lanes), bf16),
            pltpu.VMEM((shards, PAD, lanes), bf16),
            pltpu.SemaphoreType.DMA((3,)),
            pltpu.SemaphoreType.DMA((2, tasks - 1)),
            pltpu.SemaphoreType.DMA((4, shards - 1)),
        ],
        compiler_params=pltpu.CompilerParams(
            collective_id=1, has_side_effects=True, vmem_limit_bytes=VMEM_LIMIT
        ),
        name="grad_first_sum",
    )(dq, dk, dv, tokens, grad_resid, gain, w_qkv, dpk, dpv)


def last_kernel(
    grad_hbm,
    summed_ref,
    hidden_ref,
    embed_ref,
    win_hbm,
    wout_hbm,
    out_hbm,
    gembed_ref,
    gin_hbm,
    gbin_ref,
    gout_hbm,
    gbout_ref,
    win_ref,
    wout_ref,
    held,
    padded,
    gin,
    gout,
    sems,
):
    seq = out_hbm.shape[2]
    load_in = pltpu.make_async_copy(win_hbm.at[0], win_ref, sems.at[0])
    load_out = pltpu.make_async_copy(wout_hbm.at[0], wout_ref, sems.at[1])
    put_in = pltpu.make_async_copy(gin, gin_hbm.at[0], sems.at[2])
    put_out = pltpu.make_async_copy(gout, gout_hbm.at[0], sems.at[3])
    takes, puts = [], []
    for index in range(out_hbm.shape[0]):
        rows = pl.ds(index * seq, seq)
        takes.append(
            pltpu.make_async_copy(grad_hbm.at[rows, :], held.at[rows, :], sems.at[4 + 2 * index])
        )
        puts.append(
            pltpu.make_async_copy(held.at[rows, :], out_hbm.at[index, 0], sems.at[5 + 2 * index])
        )
    for load in [load_out, load_in] + takes:
        load.start()
    summed = summed_ref[...]
    hidden = hidden_ref[...]
    gout[...] = dot_tn(hidden.astype(bf16), summed)
    put_out.start()
    gbout_ref[...] = jnp.sum(summed.astype(f32), axis=0, keepdims=True)
    padded[...] = jnp.zeros(padded.shape, f32)
    padded[: embed_ref.shape[1], :] = embed_ref[0].astype(f32)
    load_out.wait()
    load_in.wait()
    grad_hidden = dot_nt(summed, wout_ref[...])
    for take, put in zip(takes, puts):
        take.wait()
        put.start()
    grad_pre = (grad_hidden * (1.0 - hidden * hidden)).astype(bf16)
    gin[...] = dot_tn(padded[...].astype(bf16), grad_pre)
    put_in.start()
    gbin_ref[...] = jnp.sum(grad_pre.astype(f32), axis=0, keepdims=True)
    gembed_ref[:, 0, :] = dot_nt(grad_pre, win_ref[...])[: embed_ref.shape[1], :]
    for copy in puts + [put_in, put_out]:
        copy.wait()


def last_call(grad, shape, summed, hidden, embed, w_in, w_out):
    width = shape[3]
    anywhere = pl.BlockSpec(memory_space=pl.ANY)
    whole = lambda shape: pl.BlockSpec(shape, lambda i: (0,) * len(shape))
    rank = w_in.shape[2]
    prefix = embed.shape[1]
    return pl.pallas_call(
        last_kernel,
        grid=(1,),
        in_specs=[anywhere]
        + [whole(x.shape) for x in (summed, hidden, embed)]
        + [anywhere, anywhere],
        out_specs=[
            anywhere,
            whole((prefix, 1, width)),
            anywhere,
            whole((1, rank)),
            anywhere,
            whole((1, 2 * width)),
        ],
        out_shape=[
            jax.ShapeDtypeStruct(shape, bf16),
            jax.ShapeDtypeStruct((prefix, 1, width), f32),
            jax.ShapeDtypeStruct(w_in.shape, f32),
            jax.ShapeDtypeStruct((1, rank), f32),
            jax.ShapeDtypeStruct(w_out.shape, f32),
            jax.ShapeDtypeStruct((1, 2 * width), f32),
        ],
        scratch_shapes=[
            pltpu.VMEM(w_in.shape[1:], bf16),
            pltpu.VMEM(w_out.shape[1:], bf16),
            pltpu.VMEM(grad.shape, bf16),
            pltpu.VMEM((PAD, width), f32),
            pltpu.VMEM(w_in.shape[1:], f32),
            pltpu.VMEM(w_out.shape[1:], f32),
            pltpu.SemaphoreType.DMA((4 + 2 * shape[0],)),
        ],
        compiler_params=pltpu.CompilerParams(vmem_limit_bytes=VMEM_LIMIT),
        name="grad_last",
    )(grad, summed, hidden, embed, w_in, w_out)


def on_device(
    tasks,
    shards,
    tokens,
    cotangent,
    segment_ids,
    task_ids,
    ln1_gain,
    ln1_bias,
    w_qkv,
    b_qkv,
    w_attn_out,
    b_attn_out,
    ln2_gain,
    ln2_bias,
    w_fc,
    b_fc,
    w_proj,
    b_proj,
    prefix_embed,
    reparam_in,
    reparam_in_bias,
    reparam_out,
    reparam_out_bias,
):
    mixed, hidden, states = qkv_call(
        tasks,
        tokens,
        ln1_gain,
        ln1_bias,
        w_qkv,
        b_qkv,
        prefix_embed,
        reparam_in,
        reparam_in_bias,
        reparam_out,
        reparam_out_bias,
    )
    probs, block_out, grad_resid, grad_attended = attention_feed_call(
        mixed,
        segment_ids,
        task_ids,
        states,
        prefix_embed.shape[1],
        tokens,
        cotangent,
        (w_attn_out, b_attn_out, ln2_gain, ln2_bias, w_fc, b_fc, w_proj, b_proj),
    )
    dq, dk, dv, dpk, dpv = attention_grad_call(mixed, states, probs, grad_attended)
    tile = 512
    first, summed = sum_call(
        tasks,
        shards,
        dq.shape[0] // tile,
        tile,
        dq,
        dk,
        dv,
        tokens,
        grad_resid,
        ln1_gain,
        w_qkv,
        dpk,
        dpv,
    )
    input_grad, gembed, gin, gbin, gout, gbout = last_call(
        first, tokens.shape, summed, hidden, prefix_embed, reparam_in, reparam_out
    )
    return (block_out, input_grad, jnp.swapaxes(gembed, 0, 1), gin, gbin, gout, gbout)


def solution(mesh):
    split = ("batch", "task")
    in_specs = (
        (P(None, split, None, None),) * 2
        + (P(None, split, None),) * 2
        + (P(),) * 12
        + (
            P("task", None, None),
            P("task", None, None),
            P("task", None),
            P("task", None, None),
            P("task", None),
        )
    )
    out_specs = (
        P(None, split, None, None),
        P(None, split, None, None),
        P("task", None, None),
        P("task", None, None),
        P("task", None),
        P("task", None, None),
        P("task", None),
    )
    return jax.shard_map(
        functools.partial(on_device, mesh.shape["task"], mesh.shape["batch"]),
        mesh=mesh,
        in_specs=in_specs,
        out_specs=out_specs,
        check_vma=False,
    )
```

```python
import functools

import jax
import jax.numpy as jnp
from jax import lax
from jax.experimental import pallas as pl
from jax.experimental.pallas import tpu as pltpu
from jax.sharding import PartitionSpec as P

bf16 = jnp.bfloat16
f32 = jnp.float32

HEADS = 16
HEAD_DIM = 64
GROUP = 4
LANES = GROUP * HEAD_DIM
QB = 64
MOST = 128
WIN = MOST + QB
PAD = 16
EPSILON = 1e-05
NEGATIVE = -1e30
LOG2E = 1.4426950408889634
LN2 = 0.6931471805599453
GELU_A = 0.7978845608028654
GELU_B = 0.044715
VMEM_LIMIT = 62 << 20
CHUNK = 32
QKV_TILE = 256
FF_CHUNK = 1024
MESH = pl.DeviceIdType.MESH


def dot_nn(left, right):
    return jnp.dot(left, right, preferred_element_type=f32)


def dot_nt(left, right):
    return lax.dot_general(
        left, right, (((1,), (1,)), ((), ())), preferred_element_type=f32
    )


def dot_tn(left, right):
    return lax.dot_general(
        left, right, (((0,), (0,)), ((), ())), preferred_element_type=f32
    )


def row_vector(ref, part=slice(None)):
    return ref[part].astype(f32)[None, :]


def normalise(hidden):
    centred = hidden - jnp.mean(hidden, axis=1, keepdims=True)
    spread = jnp.mean(centred * centred, axis=1, keepdims=True)
    inverse = lax.rsqrt(spread + EPSILON)
    return centred * inverse, inverse


def norm_backward(grad, gain, unit, inverse):
    scaled = grad * gain
    mean_one = jnp.mean(scaled, axis=1, keepdims=True)
    mean_two = jnp.mean(scaled * unit, axis=1, keepdims=True)
    return inverse * (scaled - mean_one - unit * mean_two)


def gelu_both(value, grad):
    square = value * value
    half = 0.5 + 0.5 * jnp.tanh(value * (GELU_A + (GELU_A * GELU_B) * square))
    act = value * half
    slope = half + (act * (2 * GELU_A + (6 * GELU_A * GELU_B) * square)) * (1.0 - half)
    return act.astype(bf16), (grad * slope).astype(bf16)


def barrier_with(peers):
    barrier = pltpu.get_barrier_semaphore()
    for peer in peers:
        pl.semaphore_signal(barrier, inc=1, device_id=peer, device_id_type=MESH)
    return barrier


def qkv_kernel(
    tasks,
    tok_ref,
    gain_ref,
    shift_ref,
    w_hbm,
    b_ref,
    embed_ref,
    win_hbm,
    bin_ref,
    wout_hbm,
    bout_ref,
    mixed_ref,
    hidden_ref,
    states_ref,
    win,
    wout,
    padded,
    own,
    gathered,
    w_ref,
    current,
    load_sem,
    send_sem,
    recv_sem,
):
    step = pl.program_id(0)
    last = pl.num_programs(0) - 1
    row_axis = lax.axis_index("batch")
    me = lax.axis_index("task")
    peers = [(row_axis, lax.rem(me + k, tasks)) for k in range(1, tasks)]

    width = tok_ref.shape[1]

    columns = [slice(part * width, (part + 1) * width) for part in range(3)]
    copies = [(w_hbm.at[:, part], w_ref.at[:, part]) for part in columns]
    copies += [(win_hbm.at[0], win), (wout_hbm.at[0], wout)]

    def load(index):
        return pltpu.make_async_copy(*copies[index], load_sem.at[index])

    def send(k):
        return pltpu.make_async_remote_copy(
            src_ref=own,
            dst_ref=gathered.at[me],
            send_sem=send_sem.at[k - 1],
            recv_sem=recv_sem.at[k - 1],
            device_id=peers[k - 1],
            device_id_type=MESH,
        )

    def norm():
        normed, _ = normalise(tok_ref[...].astype(f32))
        return (normed * row_vector(gain_ref) + row_vector(shift_ref)).astype(bf16)

    @pl.when(step == 0)
    def _():
        for index in range(len(copies)):
            load(index).start()
        barrier_with(peers)
        current[...] = norm()

    @pl.when(step == 2)
    def _():
        load(3).wait()
        load(4).wait()
        padded[...] = jnp.zeros(padded.shape, f32)
        padded[: embed_ref.shape[1], :] = embed_ref[0].astype(f32)
        pre = dot_nn(padded[...].astype(bf16), win[...]) + bin_ref[...].astype(f32)
        hidden = jnp.tanh(pre)
        hidden_ref[...] = hidden
        states = dot_nn(hidden.astype(bf16), wout[...]) + bout_ref[...].astype(f32)
        states = states.astype(bf16)
        own[...] = states
        gathered[me] = states
        pl.semaphore_wait(pltpu.get_barrier_semaphore(), tasks - 1)
        for k in range(1, tasks):
            send(k).start()

    def work(ready):
        following = norm()
        for index, part in enumerate(columns):
            ready(index)
            mixed = dot_nn(current[...], w_ref[:, part]) + row_vector(b_ref, part)
            if index == 0:
                mixed = mixed * (HEAD_DIM ** (-0.5) * LOG2E)
            mixed_ref[:, part] = mixed.astype(bf16)
        current[...] = following

    @pl.when(step == 1)
    def _():
        work(lambda index: load(index).wait())

    @pl.when(step > 1)
    def _():
        work(lambda index: None)

    @pl.when(step == last)
    def _():
        for k in range(1, tasks):
            send(k).wait()
        states_ref[...] = gathered[...].reshape(states_ref.shape)


def qkv_call(tasks, tokens, gain, shift, w_qkv, b_qkv, embed, w_in, b_in, w_out, b_out):
    micro, rows, seq, width = tokens.shape
    tile = QKV_TILE
    per_row = seq // tile
    rank = w_in.shape[2]
    whole1 = lambda x: pl.BlockSpec(x.shape, lambda i: (0,) * x.ndim)
    tiles = micro * rows * per_row
    ahead = lambda i: jnp.minimum(i, tiles - 1)
    return pl.pallas_call(
        functools.partial(qkv_kernel, tasks),
        grid=(tiles + 1,),
        in_specs=[
            pl.BlockSpec(
                (None, None, tile, width),
                lambda i: (
                    ahead(i) // (rows * per_row),
                    lax.rem(ahead(i) // per_row, rows),
                    lax.rem(ahead(i), per_row),
                    0,
                ),
            ),
            whole1(gain),
            whole1(shift),
            pl.BlockSpec(memory_space=pl.ANY),
            whole1(b_qkv),
            whole1(embed),
            pl.BlockSpec(memory_space=pl.ANY),
            whole1(b_in),
            pl.BlockSpec(memory_space=pl.ANY),
            whole1(b_out),
        ],
        out_specs=[
            pl.BlockSpec((tile, 3 * width), lambda i: (jnp.maximum(i - 1, 0), 0)),
            pl.BlockSpec((PAD, rank), lambda i: (0, 0)),
            pl.BlockSpec((tasks * PAD, 2 * width), lambda i: (0, 0)),
        ],
        out_shape=[
            jax.ShapeDtypeStruct((micro * rows * seq, 3 * width), bf16),
            jax.ShapeDtypeStruct((PAD, rank), f32),
            jax.ShapeDtypeStruct((tasks * PAD, 2 * width), bf16),
        ],
        scratch_shapes=[
            pltpu.VMEM(w_in.shape[1:], bf16),
            pltpu.VMEM(w_out.shape[1:], bf16),
            pltpu.VMEM((PAD, width), f32),
            pltpu.VMEM((PAD, 2 * width), bf16),
            pltpu.VMEM((tasks, PAD, 2 * width), bf16),
            pltpu.VMEM(w_qkv.shape, bf16),
            pltpu.VMEM((tile, width), bf16),
            pltpu.SemaphoreType.DMA((5,)),
            pltpu.SemaphoreType.DMA((tasks - 1,)),
            pltpu.SemaphoreType.DMA((tasks - 1,)),
        ],
        compiler_params=pltpu.CompilerParams(
            collective_id=0, has_side_effects=True, vmem_limit_bytes=VMEM_LIMIT
        ),
        name="norm_qkv",
    )(tokens, gain, shift, w_qkv, b_qkv, embed, w_in, b_in, w_out, b_out)


def stack_heads(block):
    lane = lax.broadcasted_iota(jnp.int32, (QB, 128), 1)
    zero = jnp.zeros((QB, 128), block.dtype)
    rows = []
    for h in range(GROUP):
        part = jnp.where((lane < HEAD_DIM) == (h % 2 == 0), block[:, (h // 2) * 128 :][:, :128], zero)
        rows.append(jnp.concatenate([part, zero] if h < 2 else [zero, part], axis=1))
    return jnp.concatenate(rows, axis=0)


def pick_heads(stacked):
    lane = lax.broadcasted_iota(jnp.int32, (QB, 128), 1)
    low = jnp.where(lane < HEAD_DIM, stacked[:QB, :128], stacked[QB : 2 * QB, :128])
    high = jnp.where(lane < HEAD_DIM, stacked[2 * QB : 3 * QB, 128:], stacked[3 * QB :, 128:])
    return jnp.concatenate([low, high], axis=1)


def fill_mask(seg_ref, task_ref, micro, prefix, bias, by_key):
    segments = seg_ref[...]
    seq = segments.shape[1]
    token_task = jnp.zeros(segments.shape, jnp.int32)
    for s in range(task_ref.shape[-1]):
        token_task = jnp.where(segments == s, task_ref[micro, 0, s], token_task)
    segments = segments.astype(f32)
    for c in range(0, seq, 128):
        by_key[c : c + 128, :] = jnp.broadcast_to(segments[:, c : c + 128], (128, 128)).T
    for b in range(seq // QB):
        start = max(b * QB - MOST, 0)

        def twice(x):
            part = x[:, b * QB : (b + 1) * QB]
            return jnp.concatenate([part, part], axis=1)

        key_pos = start + lax.broadcasted_iota(jnp.int32, (WIN, 128), 0)
        query_pos = b * QB + (lax.broadcasted_iota(jnp.int32, (WIN, 128), 1) & (QB - 1))
        own = (by_key[start : start + WIN, :] == twice(segments)) & (key_pos <= query_pos)
        bias[b, :WIN, :] = jnp.where(own, 0.0, NEGATIVE)
        index = lax.broadcasted_iota(jnp.int32, (bias.shape[1] - WIN, 128), 0)
        fits = (lax.shift_right_logical(index, 4) == twice(token_task)) & (
            (index & (PAD - 1)) < prefix
        )
        bias[b, WIN:, :] = jnp.where(fits, 0.0, NEGATIVE)


def own_window(block):
    start = max(block * QB - MOST, 0)
    return slice(start, start + WIN)


def fold_rows(part, combine):
    return combine(part.reshape(part.shape[0] // 8, 8, part.shape[1]), axis=0)


def skewed(items, *stages):
    for step in range(len(items) + len(stages) - 1):
        for delay, stage in enumerate(stages):
            if 0 <= step - delay < len(items):
                stage(step - delay, *items[step - delay])


def attention_feed_kernel(
    prefix,
    units,
    task_ref,
    seg_ref,
    q_ref,
    k_ref,
    v_ref,
    pk_ref,
    pv_ref,
    tok_ref,
    cot_ref,
    wa_hbm,
    ba_ref,
    gain_ref,
    shift_ref,
    wf_hbm,
    bf_ref,
    wp_hbm,
    bp_ref,
    probs_ref,
    out_ref,
    gres_ref,
    gatt_ref,
    bias,
    by_key,
    work,
    attended,
    act_all,
    gpre_all,
    wa_ref,
    wf_ref,
    wp_ref,
    weight_sem,
):
    step = pl.program_id(0)
    groups = attended.shape[1]
    unit = jnp.minimum(step, units - 1)
    micro = unit // groups
    group = lax.rem(unit, groups)
    loads = [
        pltpu.make_async_copy(source, target, weight_sem.at[index])
        for index, (source, target) in enumerate(
            ((wa_hbm, wa_ref), (wf_hbm, wf_ref), (wp_hbm, wp_ref))
        )
    ]

    for index in range(len(loads)):

        @pl.when(step == index)
        def _():
            loads[index].start()

    @pl.when((step < units) & (group == 0))
    def _():
        fill_mask(seg_ref, task_ref, micro, prefix, bias, by_key)

    pieces = [slice(c, c + CHUNK) for c in range(0, work.shape[1], CHUNK)]

    def scores(index, half, block):
        lanes = slice(half * LANES, (half + 1) * LANES)
        keys = jnp.concatenate([k_ref[own_window(block), lanes], pk_ref[:, lanes]], axis=0)
        queries = stack_heads(q_ref[block * QB : (block + 1) * QB, lanes])
        work[index % 2] = dot_nt(keys, queries)

    def softmax(index, half, block):
        slot = work.at[index % 2]
        top = None
        for piece in pieces:
            hidden = bias[block, piece, :]
            part = slot[piece, :] + jnp.concatenate([hidden, hidden], axis=1)
            slot[piece, :] = part
            part = fold_rows(part, jnp.max)
            top = part if top is None else jnp.maximum(top, part)
        top = jnp.max(top, axis=0, keepdims=True)
        total = None
        for piece in pieces:
            part = jnp.exp2(slot[piece, :] - top)
            slot[piece, :] = part
            part = fold_rows(part, jnp.sum)
            total = part if total is None else total + part
        inverse = 1.0 / jnp.sum(total, axis=0, keepdims=True)
        for piece in pieces:
            probs_ref[half, block, piece, :] = (slot[piece, :] * inverse).astype(bf16)

    def attend(index, half, block):
        lanes = slice(half * LANES, (half + 1) * LANES)
        values = jnp.concatenate([v_ref[own_window(block), lanes], pv_ref[:, lanes]], axis=0)
        result = pick_heads(dot_tn(probs_ref[half, block], values))
        attended[micro, group, block * QB : (block + 1) * QB, lanes] = result.astype(bf16)

    @pl.when(step < units)
    def _():
        items = [
            (half, block)
            for half in range(q_ref.shape[1] // LANES)
            for block in range(q_ref.shape[0] // QB)
        ]
        skewed(items, scores, softmax, attend)

    @pl.when(step == units)
    def _():
        for load in loads:
            load.wait()

    @pl.when(step >= units)
    def _():
        tile = tok_ref.shape[0]
        per_row = attended.shape[2] // tile
        index = jnp.maximum(step - units, 0)
        rows = pl.ds(pl.multiple_of(lax.rem(index, per_row) * tile, tile), tile)
        tile_attended = jnp.concatenate(
            [attended[index // per_row, g, rows, :] for g in range(groups)], axis=1
        )
        gain = row_vector(gain_ref)
        resid = tok_ref[...].astype(f32) + dot_nn(tile_attended, wa_ref[...]) + row_vector(ba_ref)
        unit_norm, inverse = normalise(resid)
        normed = (unit_norm * gain + row_vector(shift_ref)).astype(bf16)
        grad_out = cot_ref[...]
        for start in range(0, wf_ref.shape[1], FF_CHUNK):
            part = slice(start, start + FF_CHUNK)
            pre = dot_nn(normed, wf_ref[:, part]) + row_vector(bf_ref, part)
            act, gpre = gelu_both(pre, dot_nt(grad_out, wp_ref[part, :]))
            act_all[:, part] = act
            gpre_all[:, part] = gpre
        grad_normed = dot_nt(gpre_all[...], wf_ref[...])
        out = resid + dot_nn(act_all[...], wp_ref[...]) + row_vector(bp_ref)
        out_ref[...] = out.astype(bf16)
        grad_resid = grad_out.astype(f32) + norm_backward(grad_normed, gain, unit_norm, inverse)
        grad_branch = grad_resid.astype(bf16)
        gres_ref[...] = grad_branch
        gatt_ref[...] = dot_nt(grad_branch, wa_ref[...]).astype(bf16)


def attention_feed_call(
    mixed, segments, tasks, states, prefix, tokens, cotangent, weights
):
    micro, _, seq, width = tokens.shape
    groups = width // LANES
    blocks = seq // QB
    prefix_rows = states.shape[0]
    keys = WIN + prefix_rows
    both = 2
    steps = groups // both
    units = micro * steps
    tile = 256
    per_row = seq // tile
    count = micro * seq
    w_attn, _, _, _, w_fc, _, w_proj, _ = weights
    unit = lambda i: jnp.minimum(i, units - 1)
    index = lambda i: jnp.maximum(i - units, 0)
    part = lambda offset: pl.BlockSpec(
        (seq, both * LANES), lambda i: (unit(i) // steps, offset + lax.rem(unit(i), steps))
    )
    piece = lambda offset: pl.BlockSpec(
        (prefix_rows, both * LANES), lambda i: (0, offset + lax.rem(unit(i), steps))
    )
    flat = pl.BlockSpec((tile, width), lambda i: (index(i), 0))
    deep = pl.BlockSpec(
        (None, None, tile, width),
        lambda i: (index(i) // per_row, 0, lax.rem(index(i), per_row), 0),
    )

    def weight(x):
        if x.ndim == 2:
            return pl.BlockSpec(memory_space=pl.ANY)
        return pl.BlockSpec(x.shape, lambda i: (0,))

    return pl.pallas_call(
        functools.partial(attention_feed_kernel, prefix, units),
        grid=(units + count // tile,),
        in_specs=[
            pl.BlockSpec(memory_space=pltpu.SMEM),
            pl.BlockSpec((None, 1, seq), lambda i: (unit(i) // steps, 0, 0)),
            part(0),
            part(steps),
            part(2 * steps),
            piece(0),
            piece(steps),
            deep,
            deep,
        ]
        + [weight(x) for x in weights],
        out_specs=[
            pl.BlockSpec(
                (None, both, blocks, keys, LANES),
                lambda i: (unit(i) // steps, lax.rem(unit(i), steps), 0, 0, 0),
            ),
            deep,
            flat,
            flat,
        ],
        out_shape=[
            jax.ShapeDtypeStruct((micro, groups, blocks, keys, LANES), bf16),
            jax.ShapeDtypeStruct(tokens.shape, bf16),
            jax.ShapeDtypeStruct((count, width), bf16),
            jax.ShapeDtypeStruct((count, width), bf16),
        ],
        scratch_shapes=[
            pltpu.VMEM((blocks, keys, 128), f32),
            pltpu.VMEM((seq, 128), f32),
            pltpu.VMEM((2, keys, LANES), f32),
            pltpu.VMEM((micro, steps, seq, both * LANES), bf16),
            pltpu.VMEM((tile, w_fc.shape[1]), bf16),
            pltpu.VMEM((tile, w_fc.shape[1]), bf16),
        ]
        + [pltpu.VMEM(x.shape, bf16) for x in (w_attn, w_fc, w_proj)]
        + [pltpu.SemaphoreType.DMA((3,))],
        compiler_params=pltpu.CompilerParams(vmem_limit_bytes=VMEM_LIMIT),
        name="attention_feed",
    )(tasks, segments, mixed, mixed, mixed, states, states, tokens, cotangent, *weights)


def attention_grad_kernel(
    q_ref,
    k_ref,
    v_ref,
    pk_ref,
    pv_ref,
    probs_ref,
    g_ref,
    dq_ref,
    dk_ref,
    dv_ref,
    dpk_ref,
    dpv_ref,
    key_sum,
    value_sum,
    prefix_key_sum,
    prefix_value_sum,
    work,
    score_grad,
):
    blocks = q_ref.shape[0] // QB
    pieces = [slice(c, c + CHUNK) for c in range(0, work.shape[1], CHUNK)]

    def prob_grads(index, block):
        values = jnp.concatenate([v_ref[own_window(block), :], pv_ref[...]], axis=0)
        grads = stack_heads(g_ref[block * QB : (block + 1) * QB, :])
        work[index % 2] = dot_nt(values, grads)

    def softmax_grads(index, block):
        slot = work.at[index % 2]
        delta = None
        for piece in pieces:
            part = slot[piece, :] * probs_ref[block, piece, :].astype(f32)
            slot[piece, :] = part
            part = fold_rows(part, jnp.sum)
            delta = part if delta is None else delta + part
        delta = jnp.sum(delta, axis=0, keepdims=True)
        for piece in pieces:
            part = slot[piece, :] - probs_ref[block, piece, :].astype(f32) * delta
            score_grad[index % 2, piece, :] = part.astype(bf16)

    def mixed_grads(index, block):
        rows = slice(block * QB, (block + 1) * QB)
        window = own_window(block)
        keys = jnp.concatenate([k_ref[window, :], pk_ref[...]], axis=0)
        back = score_grad[index % 2]
        dv = dot_nn(probs_ref[block], stack_heads(g_ref[rows, :]))
        dk = dot_nn(back, stack_heads(q_ref[rows, :]))
        dq = pick_heads(dot_tn(back, keys))
        dq_ref[rows, :] = (dq * HEAD_DIM ** (-0.5)).astype(bf16)
        start = window.start
        old = 0 if block == 0 else block * QB - start if start else WIN
        for total, fresh in ((key_sum, dk), (value_sum, dv)):
            if old:
                total[start : start + old, :] += fresh[:old]
            if old < WIN:
                total[start + old : start + WIN, :] = fresh[old:WIN]
        for total, fresh in ((prefix_key_sum, dk), (prefix_value_sum, dv)):
            if block == 0:
                total[...] = fresh[WIN:]
            else:
                total[...] += fresh[WIN:]
        done = slice(start, window.stop if block == blocks - 1 else start + QB if block >= 2 else 0)
        if done.stop > done.start:
            dk_ref[done, :] = (key_sum[done, :] * LN2).astype(bf16)
            dv_ref[done, :] = value_sum[done, :].astype(bf16)

    skewed([(block,) for block in range(blocks)], prob_grads, softmax_grads, mixed_grads)

    @pl.when(pl.program_id(1) == 0)
    def _():
        dpk_ref[...] = prefix_key_sum[...] * LN2
        dpv_ref[...] = prefix_value_sum[...]

    @pl.when(pl.program_id(1) != 0)
    def _():
        dpk_ref[...] += prefix_key_sum[...] * LN2
        dpv_ref[...] += prefix_value_sum[...]


def attention_grad_call(mixed, states, probs, grad_attended):
    micro, groups, blocks, keys, _ = probs.shape
    seq = blocks * QB
    width = grad_attended.shape[1]
    prefix_rows = states.shape[0]
    part = lambda offset: pl.BlockSpec((seq, LANES), lambda g, r: (r, offset + g))
    piece = lambda offset: pl.BlockSpec((prefix_rows, LANES), lambda g, r: (0, offset + g))
    return pl.pallas_call(
        attention_grad_kernel,
        grid=(groups, micro),
        in_specs=[
            part(0),
            part(groups),
            part(2 * groups),
            piece(0),
            piece(groups),
            pl.BlockSpec((None, None, blocks, keys, LANES), lambda g, r: (r, g, 0, 0, 0)),
            part(0),
        ],
        out_specs=[part(0)] * 3 + [piece(0)] * 2,
        out_shape=[jax.ShapeDtypeStruct((micro * seq, width), bf16)] * 3
        + [jax.ShapeDtypeStruct((prefix_rows, width), f32)] * 2,
        scratch_shapes=[pltpu.VMEM((seq, LANES), f32)] * 2
        + [pltpu.VMEM((prefix_rows, LANES), f32)] * 2
        + [pltpu.VMEM((2, keys, LANES), f32), pltpu.VMEM((2, keys, LANES), bf16)],
        compiler_params=pltpu.CompilerParams(vmem_limit_bytes=VMEM_LIMIT),
        name="attention_grad",
    )(mixed, mixed, mixed, states, states, probs, grad_attended)


def sum_kernel(
    tasks,
    shards,
    dq_ref,
    dk_ref,
    dv_ref,
    tok_ref,
    gres_ref,
    gain_ref,
    w_hbm,
    dpk_ref,
    dpv_ref,
    grad_ref,
    summed_ref,
    w_ref,
    send_a,
    recv_a,
    send_b,
    recv_b,
    gathered,
    load_sem,
    sems,
    sems_b,
):
    step = pl.program_id(0)
    last = pl.num_programs(0) - 1
    shard = lax.axis_index("batch")
    task = lax.axis_index("task")
    task_peers = [(shard, lax.rem(task + k, tasks)) for k in range(1, tasks)]
    shard_peers = [(lax.rem(shard + k, shards), task) for k in range(1, shards)]
    width = dpk_ref.shape[1]
    lanes = send_b.shape[2]
    loads = [
        pltpu.make_async_copy(
            w_hbm.at[:, index * width : (index + 1) * width],
            w_ref.at[:, index * width : (index + 1) * width],
            load_sem.at[index],
        )
        for index in range(3)
    ]

    def to_task(k):
        return pltpu.make_async_remote_copy(
            src_ref=send_a.at[lax.rem(task + k, tasks)],
            dst_ref=recv_a.at[k - 1],
            send_sem=sems.at[0, k - 1],
            recv_sem=sems.at[1, k - 1],
            device_id=task_peers[k - 1],
            device_id_type=MESH,
        )

    def to_shard(k):
        return pltpu.make_async_remote_copy(
            src_ref=send_b.at[lax.rem(shard + k, shards)],
            dst_ref=recv_b.at[k - 1],
            send_sem=sems_b.at[0, k - 1],
            recv_sem=sems_b.at[1, k - 1],
            device_id=shard_peers[k - 1],
            device_id_type=MESH,
        )

    def back_to_shard(k):
        return pltpu.make_async_remote_copy(
            src_ref=gathered.at[shard],
            dst_ref=gathered.at[shard],
            send_sem=sems_b.at[2, k - 1],
            recv_sem=sems_b.at[3, k - 1],
            device_id=shard_peers[k - 1],
            device_id_type=MESH,
        )

    def start_tasks():
        pl.semaphore_wait(pltpu.get_barrier_semaphore(), tasks - 1 + shards - 1)
        for k in range(1, tasks):
            to_task(k).start()

    def start_shards():
        for k in range(1, tasks):
            to_task(k).wait()
        total = send_a[task].astype(f32)
        for k in range(1, tasks):
            total = total + recv_a[k - 1].astype(f32)
        total = total.astype(bf16)
        for c in range(shards):
            send_b[c] = total[:, c * lanes : (c + 1) * lanes]
        for k in range(1, shards):
            to_shard(k).start()

    def start_back():
        for k in range(1, shards):
            to_shard(k).wait()
        total = send_b[shard].astype(f32)
        for k in range(1, shards):
            total = total + recv_b[k - 1].astype(f32)
        gathered[shard] = total.astype(bf16)
        for k in range(1, shards):
            back_to_shard(k).start()

    @pl.when(step == 0)
    def _():
        for load in loads:
            load.start()
        barrier_with(task_peers + shard_peers)
        for t in range(tasks):
            part = slice(t * PAD, (t + 1) * PAD)
            send_a[t, :, :width] = dpk_ref[part, :].astype(bf16)
            send_a[t, :, width:] = dpv_ref[part, :].astype(bf16)

    @pl.when(step == 1)
    def _():
        start_tasks()

    @pl.when(step == 2)
    def _():
        start_shards()

    @pl.when(step == 3)
    def _():
        start_back()

    def work(ready):
        grad = 0.0
        for index, part in enumerate((dq_ref, dk_ref, dv_ref)):
            ready(index)
            grad = grad + dot_nt(part[...], w_ref[:, index * width : (index + 1) * width])
        unit, inverse = normalise(tok_ref[...].astype(f32))
        back = norm_backward(grad, row_vector(gain_ref), unit, inverse)
        grad_ref[...] = (gres_ref[...].astype(f32) + back).astype(bf16)

    @pl.when(step == 0)
    def _():
        work(lambda index: loads[index].wait())

    @pl.when(step > 0)
    def _():
        work(lambda index: None)

    @pl.when(step == last)
    def _():
        for k in range(1, shards):
            back_to_shard(k).wait()
        for c in range(shards):
            summed_ref[:, c * lanes : (c + 1) * lanes] = gathered[c]


def sum_call(tasks, shards, tiles, tile, dq, dk, dv, tokens, grad_resid, gain, w_qkv, dpk, dpv):
    seq, width = tokens.shape[2:]
    per_row = seq // tile
    assert tiles >= 4
    flat = pl.BlockSpec((tile, width), lambda i: (i, 0))
    lanes = 2 * width // shards
    whole = lambda x: pl.BlockSpec(x.shape, lambda i: (0,) * x.ndim)
    return pl.pallas_call(
        functools.partial(sum_kernel, tasks, shards),
        grid=(tiles,),
        in_specs=[flat, flat, flat]
        + [
            pl.BlockSpec((None, None, tile, width), lambda i: (i // per_row, 0, i % per_row, 0)),
            flat,
            whole(gain),
            pl.BlockSpec(memory_space=pl.ANY),
            whole(dpk),
            whole(dpv),
        ],
        out_specs=[flat, pl.BlockSpec((PAD, 2 * width), lambda i: (0, 0))],
        out_shape=[
            jax.ShapeDtypeStruct((tiles * tile, width), bf16),
            jax.ShapeDtypeStruct((PAD, 2 * width), bf16),
        ],
        scratch_shapes=[
            pltpu.VMEM(w_qkv.shape, bf16),
            pltpu.VMEM((tasks, PAD, 2 * width), bf16),
            pltpu.VMEM((tasks - 1, PAD, 2 * width), bf16),
            pltpu.VMEM((shards, PAD, lanes), bf16),
            pltpu.VMEM((shards - 1, PAD, lanes), bf16),
            pltpu.VMEM((shards, PAD, lanes), bf16),
            pltpu.SemaphoreType.DMA((3,)),
            pltpu.SemaphoreType.DMA((2, tasks - 1)),
            pltpu.SemaphoreType.DMA((4, shards - 1)),
        ],
        compiler_params=pltpu.CompilerParams(
            collective_id=1, has_side_effects=True, vmem_limit_bytes=VMEM_LIMIT
        ),
        name="grad_first_sum",
    )(dq, dk, dv, tokens, grad_resid, gain, w_qkv, dpk, dpv)


def last_kernel(
    grad_hbm,
    summed_ref,
    hidden_ref,
    embed_ref,
    win_hbm,
    wout_hbm,
    out_hbm,
    gembed_ref,
    gin_hbm,
    gbin_ref,
    gout_hbm,
    gbout_ref,
    win_ref,
    wout_ref,
    held,
    padded,
    gin,
    gout,
    sems,
):
    seq = out_hbm.shape[2]
    load_in = pltpu.make_async_copy(win_hbm.at[0], win_ref, sems.at[0])
    load_out = pltpu.make_async_copy(wout_hbm.at[0], wout_ref, sems.at[1])
    put_in = pltpu.make_async_copy(gin, gin_hbm.at[0], sems.at[2])
    put_out = pltpu.make_async_copy(gout, gout_hbm.at[0], sems.at[3])
    takes, puts = [], []
    for index in range(out_hbm.shape[0]):
        rows = pl.ds(index * seq, seq)
        takes.append(
            pltpu.make_async_copy(grad_hbm.at[rows, :], held.at[rows, :], sems.at[4 + 2 * index])
        )
        puts.append(
            pltpu.make_async_copy(held.at[rows, :], out_hbm.at[index, 0], sems.at[5 + 2 * index])
        )
    for load in [load_out, load_in] + takes:
        load.start()
    summed = summed_ref[...]
    hidden = hidden_ref[...]
    gout[...] = dot_tn(hidden.astype(bf16), summed)
    put_out.start()
    gbout_ref[...] = jnp.sum(summed.astype(f32), axis=0, keepdims=True)
    padded[...] = jnp.zeros(padded.shape, f32)
    padded[: embed_ref.shape[1], :] = embed_ref[0].astype(f32)
    load_out.wait()
    load_in.wait()
    grad_hidden = dot_nt(summed, wout_ref[...])
    for take, put in zip(takes, puts):
        take.wait()
        put.start()
    grad_pre = (grad_hidden * (1.0 - hidden * hidden)).astype(bf16)
    gin[...] = dot_tn(padded[...].astype(bf16), grad_pre)
    put_in.start()
    gbin_ref[...] = jnp.sum(grad_pre.astype(f32), axis=0, keepdims=True)
    gembed_ref[:, 0, :] = dot_nt(grad_pre, win_ref[...])[: embed_ref.shape[1], :]
    for copy in puts + [put_in, put_out]:
        copy.wait()


def last_call(grad, shape, summed, hidden, embed, w_in, w_out):
    width = shape[3]
    anywhere = pl.BlockSpec(memory_space=pl.ANY)
    whole = lambda shape: pl.BlockSpec(shape, lambda i: (0,) * len(shape))
    rank = w_in.shape[2]
    prefix = embed.shape[1]
    return pl.pallas_call(
        last_kernel,
        grid=(1,),
        in_specs=[anywhere]
        + [whole(x.shape) for x in (summed, hidden, embed)]
        + [anywhere, anywhere],
        out_specs=[
            anywhere,
            whole((prefix, 1, width)),
            anywhere,
            whole((1, rank)),
            anywhere,
            whole((1, 2 * width)),
        ],
        out_shape=[
            jax.ShapeDtypeStruct(shape, bf16),
            jax.ShapeDtypeStruct((prefix, 1, width), f32),
            jax.ShapeDtypeStruct(w_in.shape, f32),
            jax.ShapeDtypeStruct((1, rank), f32),
            jax.ShapeDtypeStruct(w_out.shape, f32),
            jax.ShapeDtypeStruct((1, 2 * width), f32),
        ],
        scratch_shapes=[
            pltpu.VMEM(w_in.shape[1:], bf16),
            pltpu.VMEM(w_out.shape[1:], bf16),
            pltpu.VMEM(grad.shape, bf16),
            pltpu.VMEM((PAD, width), f32),
            pltpu.VMEM(w_in.shape[1:], f32),
            pltpu.VMEM(w_out.shape[1:], f32),
            pltpu.SemaphoreType.DMA((4 + 2 * shape[0],)),
        ],
        compiler_params=pltpu.CompilerParams(vmem_limit_bytes=VMEM_LIMIT),
        name="grad_last",
    )(grad, summed, hidden, embed, w_in, w_out)


def on_device(
    tasks,
    shards,
    tokens,
    cotangent,
    segment_ids,
    task_ids,
    ln1_gain,
    ln1_bias,
    w_qkv,
    b_qkv,
    w_attn_out,
    b_attn_out,
    ln2_gain,
    ln2_bias,
    w_fc,
    b_fc,
    w_proj,
    b_proj,
    prefix_embed,
    reparam_in,
    reparam_in_bias,
    reparam_out,
    reparam_out_bias,
):
    mixed, hidden, states = qkv_call(
        tasks,
        tokens,
        ln1_gain,
        ln1_bias,
        w_qkv,
        b_qkv,
        prefix_embed,
        reparam_in,
        reparam_in_bias,
        reparam_out,
        reparam_out_bias,
    )
    probs, block_out, grad_resid, grad_attended = attention_feed_call(
        mixed,
        segment_ids,
        task_ids,
        states,
        prefix_embed.shape[1],
        tokens,
        cotangent,
        (w_attn_out, b_attn_out, ln2_gain, ln2_bias, w_fc, b_fc, w_proj, b_proj),
    )
    dq, dk, dv, dpk, dpv = attention_grad_call(mixed, states, probs, grad_attended)
    tile = 512
    first, summed = sum_call(
        tasks,
        shards,
        dq.shape[0] // tile,
        tile,
        dq,
        dk,
        dv,
        tokens,
        grad_resid,
        ln1_gain,
        w_qkv,
        dpk,
        dpv,
    )
    input_grad, gembed, gin, gbin, gout, gbout = last_call(
        first, tokens.shape, summed, hidden, prefix_embed, reparam_in, reparam_out
    )
    return (block_out, input_grad, jnp.swapaxes(gembed, 0, 1), gin, gbin, gout, gbout)


def solution(mesh):
    split = ("batch", "task")
    in_specs = (
        (P(None, split, None, None),) * 2
        + (P(None, split, None),) * 2
        + (P(),) * 12
        + (
            P("task", None, None),
            P("task", None, None),
            P("task", None),
            P("task", None, None),
            P("task", None),
        )
    )
    out_specs = (
        P(None, split, None, None),
        P(None, split, None, None),
        P("task", None, None),
        P("task", None, None),
        P("task", None),
        P("task", None, None),
        P("task", None),
    )
    return jax.shard_map(
        functools.partial(on_device, mesh.shape["task"], mesh.shape["batch"]),
        mesh=mesh,
        in_specs=in_specs,
        out_specs=out_specs,
        check_vma=False,
    )
```
